32 devices in a mesh: dp: 16 (over z, y, x), mp: 2 (over core).
Axes of the slice: x: 2, y: 2, z: 4, core: 2. Of those that a mesh axis runs over, the one named last changes fastest.
Arguments:
- context: bfloat16 [1536, 1024], P('dp'), may hold values from -6 to 6
- codes: int32 [1536, 3, 2], P('dp'), may hold values from 0 to 2047
- delays: int32 [1536], P('dp'), may hold values from 1 to 2
- counts: int32 [1536], P('dp'), may hold values from 0 to 2, as said below
- w_attn_in: float32 [2, 1024, 3, 1024], P(None, 'dp', None, 'mp'), may hold values from -0.1875 to 0.1875
- w_attn_out: float32 [2, 1024, 1024], P(None, 'mp', 'dp'), may hold values from -0.25 to 0.25
- w_gate_up: float32 [2, 1024, 2, 2816], P(None, 'dp', None, 'mp'), may hold values from -0.1875 to 0.1875
- w_down: float32 [2, 2816, 1024], P(None, 'mp', 'dp'), may hold values from -0.109375 to 0.109375
- w_head: float32 [2, 1024, 2048], P(None, 'dp', 'mp'), may hold values from -0.375 to 0.375
- embed_table: float32 [1, 2048, 1024], P(None, 'mp', 'dp'), may hold values from -6 to 6
- norm_gains: float32 [2, 3, 1024], P(None, None, 'dp'), may hold values from 0.5 to 1.5
- first_attn_in: float32 [2, 1024, 3, 1024], P(None, 'dp', None, 'mp'), may hold values from -2.3841858e-06 to 2.3841858e-06
- first_attn_out: float32 [2, 1024, 1024], P(None, 'mp', 'dp'), may hold values from -2.3841858e-06 to 2.3841858e-06
- first_gate_up: float32 [2, 1024, 2, 2816], P(None, 'dp', None, 'mp'), may hold values from -2.3841858e-06 to 2.3841858e-06
- first_down: float32 [2, 2816, 1024], P(None, 'mp', 'dp'), may hold values from -2.3841858e-06 to 2.3841858e-06
- first_head: float32 [2, 1024, 2048], P(None, 'dp', 'mp'), may hold values from -2.3841858e-06 to 2.3841858e-06
- first_embed: float32 [1, 2048, 1024], P(None, 'mp', 'dp'), may hold values from -2.3841858e-07 to 2.3841858e-07
- first_gains: float32 [2, 3, 1024], P(None, None, 'dp'), may hold values from -7.6293945e-06 to 7.6293945e-06
- second_attn_in: float32 [2, 1024, 3, 1024], P(None, 'dp', None, 'mp'), may hold values from 6.252401e-13 to 2.5009604e-12
- second_attn_out: float32 [2, 1024, 1024], P(None, 'mp', 'dp'), may hold values from 6.252401e-13 to 2.5009604e-12
- second_gate_up: float32 [2, 1024, 2, 2816], P(None, 'dp', None, 'mp'), may hold values from 6.252401e-13 to 2.5009604e-12
- second_down: float32 [2, 2816, 1024], P(None, 'mp', 'dp'), may hold values from 6.252401e-13 to 2.5009604e-12
- second_head: float32 [2, 1024, 2048], P(None, 'dp', 'mp'), may hold values from 6.252401e-13 to 2.5009604e-12
- second_embed: float32 [1, 2048, 1024], P(None, 'mp', 'dp'), may hold values from 6.252401e-15 to 2.5009603e-14
- second_gains: float32 [2, 3, 1024], P(None, None, 'dp'), may hold values from 6.252401e-12 to 2.5009604e-11
Outputs:
- next_attn_in: float32 [2, 1024, 3, 1024], P(None, 'dp', None, 'mp')
- next_attn_out: float32 [2, 1024, 1024], P(None, 'mp', 'dp')
- next_gate_up: float32 [2, 1024, 2, 2816], P(None, 'dp', None, 'mp')
- next_down: float32 [2, 2816, 1024], P(None, 'mp', 'dp')
- next_head: float32 [2, 1024, 2048], P(None, 'dp', 'mp')
- next_embed: float32 [1, 2048, 1024], P(None, 'mp', 'dp')
- next_gains: float32 [2, 3, 1024], P(None, None, 'dp')
- next_first_attn_in: float32 [2, 1024, 3, 1024], P(None, 'dp', None, 'mp')
- next_first_attn_out: float32 [2, 1024, 1024], P(None, 'mp', 'dp')
- next_first_gate_up: float32 [2, 1024, 2, 2816], P(None, 'dp', None, 'mp')
- next_first_down: float32 [2, 2816, 1024], P(None, 'mp', 'dp')
- next_first_head: float32 [2, 1024, 2048], P(None, 'dp', 'mp')
- next_first_embed: float32 [1, 2048, 1024], P(None, 'mp', 'dp')
- next_first_gains: float32 [2, 3, 1024], P(None, None, 'dp')
- next_second_attn_in: float32 [2, 1024, 3, 1024], P(None, 'dp', None, 'mp')
- next_second_attn_out: float32 [2, 1024, 1024], P(None, 'mp', 'dp')
- next_second_gate_up: float32 [2, 1024, 2, 2816], P(None, 'dp', None, 'mp')
- next_second_down: float32 [2, 2816, 1024], P(None, 'mp', 'dp')
- next_second_head: float32 [2, 1024, 2048], P(None, 'dp', 'mp')
- next_second_embed: float32 [1, 2048, 1024], P(None, 'mp', 'dp')
- next_second_gains: float32 [2, 3, 1024], P(None, None, 'dp')
- loss: float32 [], replicated
- grad_norm: float32 [], replicated
The draws below stay inside these ranges and needn't reach their ends.
Inputs may be any that keep to these rules, and one draw needn't show every extreme that they name: Positions 0 to counts - 1 of a frame count in the loss.
All inputs are finite; a program needn't handle non-finite values.
Results may differ from the reference program's by a relative error of at most 0.012.
Values may be sent and summed in bfloat16 or wider, within the bound.
No kernel may reach another device: no remote copies, remote signals or barrier semaphores. Data moves between devices by JAX's collectives and lax.ppermute only.
A program may use at most 256 MiB of HBM per device.

```python
import math
import jax
import jax.numpy as jnp
from jax import lax

D = 1024
HEAD_DIM = 64
FF = 2816
V = 2048
CB = 2
FR_DEV = 96
FRAMES = 1536
PARAMS = 31987712


def draw_counts(key, part):
    key_one, key_two = jax.random.split(key)
    frame_ids = lax.broadcasted_iota(jnp.int32, (FRAMES,), 0)
    blocks = FRAMES // FR_DEV
    owner_rank = frame_ids // FR_DEV
    base_span = max(blocks - 1, 1)
    lottery = jax.random.randint(key_one, (FRAMES,), 0, 3 * base_span)
    length = jax.random.randint(key_two, (FRAMES,), 1, CB + 1)
    drawn = jnp.where(lottery < base_span + 2 * owner_rank, length, 0)
    drawn = jnp.where(frame_ids == 0, 0, drawn)
    return jnp.where(frame_ids == FRAMES - 1, CB, drawn).astype(jnp.int32)


def place_ends(entries, rng, low, largest):
    dims = entries.shape
    place = [jax.random.randint(jax.random.fold_in(rng, axis), (), 0, dims[axis]) for axis in range(len(dims))]
    entries = entries.at[tuple(place)].set(low)
    longest = dims.index(max(dims))
    place[longest] = (place[longest] + 1) % dims[longest]
    return entries.at[tuple(place)].set(largest)


def block_scale(rng, extent, cuts, least, largest):
    factor_of = 1.0
    for dim, parts in cuts:
        heights = jax.random.uniform(jax.random.fold_in(jax.random.fold_in(rng, 6), dim), (parts,), jnp.float32, least / len(cuts), largest / len(cuts))
        factor_of = factor_of * jnp.repeat(jnp.exp(heights), extent[dim] // parts).reshape((-1,) + (1,) * (len(extent) - 1 - dim))
    return factor_of


def noise(key, shape, deviation, bound, cuts=(), held_as=jnp.bfloat16):
    result = deviation * jax.random.normal(key, shape, jnp.float32)
    if cuts:
        result = result * block_scale(key, shape, cuts, -0.22, 0.18)
    return jnp.clip(result, -bound, bound).astype(held_as)


def setup_inputs(seed: int = 0) -> dict:
    streams_of = jax.random.split(jax.random.key(seed), 26)
    return {
        "context": noise(streams_of[0], (FRAMES, D), 1.0, 6.0, ((0, 16),)),
        "codes": place_ends(jax.random.randint(streams_of[1], (FRAMES, 3, CB), 0, V), jax.random.fold_in(streams_of[1], 1), 0, V - 1).astype(jnp.int32),
        "delays": place_ends(jax.random.randint(streams_of[2], (FRAMES,), 1, 3), jax.random.fold_in(streams_of[2], 1), 1, 2).astype(jnp.int32),
        "counts": draw_counts(jax.random.fold_in(streams_of[25], 71), 0),
        "w_attn_in": noise(streams_of[4], (CB, D, 3, D), D ** -0.5, 0.1875, ((1, 16), (3, 2)), jnp.float32),
        "w_attn_out": noise(streams_of[5], (CB, D, D), (D // 2) ** -0.5, 0.25, ((1, 2), (2, 16)), jnp.float32),
        "w_gate_up": noise(streams_of[6], (CB, D, 2, FF), D ** -0.5, 0.1875, ((1, 16), (3, 2)), jnp.float32),
        "w_down": noise(streams_of[7], (CB, FF, D), FF ** -0.5, 0.109375, ((1, 2), (2, 16)), jnp.float32),
        "w_head": noise(streams_of[8], (CB, D, V), (D // 4) ** -0.5, 0.375, ((1, 16), (2, 2)), jnp.float32),
        "embed_table": noise(streams_of[9], (CB - 1, V, D), 1.0, 6.0, ((1, 2), (2, 16)), jnp.float32),
        "norm_gains": jnp.clip(1.0 + 0.1 * jax.random.normal(streams_of[10], (CB, 3, D), jnp.float32), 0.5, 1.5),
        "first_attn_in": noise(streams_of[11], (CB, D, 3, D), (0.00222 * PARAMS ** -0.5), 2.384185791015625e-06, ((1, 16), (3, 2)), jnp.float32),
        "first_attn_out": noise(streams_of[12], (CB, D, D), (0.00222 * PARAMS ** -0.5), 2.384185791015625e-06, ((1, 2), (2, 16)), jnp.float32),
        "first_gate_up": noise(streams_of[13], (CB, D, 2, FF), (0.00222 * PARAMS ** -0.5), 2.384185791015625e-06, ((1, 16), (3, 2)), jnp.float32),
        "first_down": noise(streams_of[14], (CB, FF, D), (0.00222 * PARAMS ** -0.5), 2.384185791015625e-06, ((1, 2), (2, 16)), jnp.float32),
        "first_head": noise(streams_of[15], (CB, D, V), (0.00222 * PARAMS ** -0.5), 2.384185791015625e-06, ((1, 16), (2, 2)), jnp.float32),
        "first_embed": noise(streams_of[16], (CB - 1, V, D), (0.000222 * PARAMS ** -0.5), 2.384185791015625e-07, ((1, 2), (2, 16)), jnp.float32),
        "first_gains": noise(streams_of[17], (CB, 3, D), (0.00666 * PARAMS ** -0.5), 7.62939453125e-06, ((2, 16),), jnp.float32),
        "second_attn_in": jnp.clip(jnp.exp(math.log(2.5009603762948807e-12) - 1.3862944 * jax.random.uniform(streams_of[18], (CB, D, 3, D), jnp.float32) ** block_scale(streams_of[18], (CB, D, 3, D), ((1, 16), (3, 2)), -0.2, 0.2)), 6.252400940737202e-13, 2.5009603762948807e-12),
        "second_attn_out": jnp.clip(jnp.exp(math.log(2.5009603762948807e-12) - 1.3862944 * jax.random.uniform(streams_of[19], (CB, D, D), jnp.float32) ** block_scale(streams_of[19], (CB, D, D), ((1, 2), (2, 16)), -0.2, 0.2)), 6.252400940737202e-13, 2.5009603762948807e-12),
        "second_gate_up": jnp.clip(jnp.exp(math.log(2.5009603762948807e-12) - 1.3862944 * jax.random.uniform(streams_of[20], (CB, D, 2, FF), jnp.float32) ** block_scale(streams_of[20], (CB, D, 2, FF), ((1, 16), (3, 2)), -0.2, 0.2)), 6.252400940737202e-13, 2.5009603762948807e-12),
        "second_down": jnp.clip(jnp.exp(math.log(2.5009603762948807e-12) - 1.3862944 * jax.random.uniform(streams_of[21], (CB, FF, D), jnp.float32) ** block_scale(streams_of[21], (CB, FF, D), ((1, 2), (2, 16)), -0.2, 0.2)), 6.252400940737202e-13, 2.5009603762948807e-12),
        "second_head": jnp.clip(jnp.exp(math.log(2.5009603762948807e-12) - 1.3862944 * jax.random.uniform(streams_of[22], (CB, D, V), jnp.float32) ** block_scale(streams_of[22], (CB, D, V), ((1, 16), (2, 2)), -0.2, 0.2)), 6.252400940737202e-13, 2.5009603762948807e-12),
        "second_embed": jnp.clip(jnp.exp(math.log(2.500960322084772e-14) - 1.3862944 * jax.random.uniform(streams_of[23], (CB - 1, V, D), jnp.float32) ** block_scale(streams_of[23], (CB - 1, V, D), ((1, 2), (2, 16)), -0.2, 0.2)), 6.25240080521193e-15, 2.500960322084772e-14),
        "second_gains": jnp.clip(jnp.exp(math.log(2.5009603762948807e-11) - 1.3862944 * jax.random.uniform(streams_of[24], (CB, 3, D), jnp.float32) ** block_scale(streams_of[24], (CB, 3, D), ((2, 16),), -0.2, 0.2)), 6.252400940737202e-12, 2.5009603762948807e-11),
    }


HIGH = lax.Precision.HIGHEST
NORM_EPS = 1e-05
CLIP_NORM = 0.02
BETA_ONE = 0.9
BETA_TWO = 0.95
BIAS_ONE = 1.0 - 0.9 ** 10
BIAS_TWO = 1.0 - 0.95 ** 10
ADAM_EPS = 1e-08
DECAY = 0.1
RATE_MATRIX = 0.03
RATE_TABLE = 0.5

@jax.custom_vjp
def low(v):
    return lax.optimization_barrier(v.astype(jnp.bfloat16)).astype(jnp.float32)

@jax.custom_vjp
def low_back(v):
    return v

def low_keep(v):
    return (low(v), None)

def low_pass(kept, grad):
    return (grad,)

def back_keep(v):
    return (v, None)

def back_low(kept, grad):
    return (low(grad),)
low.defvjp(low_keep, low_pass)
low_back.defvjp(back_keep, back_low)

def both_round(value):
    return low(low_back(value))

def rms_norm(inputs, gain_vec):
    return inputs * lax.rsqrt(lax.optimization_barrier(jnp.mean(inputs * inputs, axis=-1, keepdims=True)) + NORM_EPS) * gain_vec

def attend(queries, key_vecs, values):
    scores = jnp.einsum('kfhd,jfhd->fhkj', queries, key_vecs, precision=HIGH) * 0.125
    num_pos = queries.shape[0]
    causal = lax.broadcasted_iota(jnp.int32, (num_pos, num_pos), 0) >= lax.broadcasted_iota(jnp.int32, (num_pos, num_pos), 1)
    scores = jnp.where(causal, scores, -1e+30)
    probs = jax.nn.softmax(scores, axis=-1)
    mixture = jnp.einsum('fhkj,jfhd->kfhd', probs, values, precision=HIGH)
    return mixture.reshape(mixture.shape[0], mixture.shape[1], -1)

def pick_targets(codes, delays):
    window = lax.broadcasted_iota(jnp.int32, (1, codes.shape[1], 1), 1)
    delayed = lax.optimization_barrier(jnp.sum(jnp.where(window == delays[:, None, None], codes, 0), axis=1))
    position = lax.broadcasted_iota(jnp.int32, delayed.shape, 1)
    return jnp.where(position == 0, codes[:, 0, :], delayed)

def block_loss(weights, context, targets, loss_mask):
    w_attn_in, w_attn_out, w_gate_up, w_down, w_head, embed_table, norm_gains = (low(weight) for weight in weights)
    by_pos = targets.T
    table_ids = jnp.arange(embed_table.shape[0])[:, None]
    looked = low_back(embed_table[table_ids, by_pos[:-1]])
    stream = jnp.concatenate([context.astype(jnp.float32)[None], looked], axis=0)
    attn_in = rms_norm(stream, norm_gains[:, 0:1, :])
    qkv = both_round(jnp.einsum('kfd,kdce->kfce', low(attn_in), w_attn_in, precision=HIGH))
    head_shape = qkv.shape[:2] + (qkv.shape[3] // HEAD_DIM, HEAD_DIM)
    attended = low(attend(qkv[:, :, 0].reshape(head_shape), qkv[:, :, 1].reshape(head_shape), qkv[:, :, 2].reshape(head_shape)))
    residual = stream + low_back(jnp.einsum('kfi,kio->kfo', attended, w_attn_out, precision=HIGH))
    ffn_in = rms_norm(residual, norm_gains[:, 1:2, :])
    gate_up = low_back(jnp.einsum('kfd,kdch->kfch', low(ffn_in), w_gate_up, precision=HIGH))
    hidden = low(jax.nn.silu(gate_up[:, :, 0]) * gate_up[:, :, 1])
    output = residual + low_back(jnp.einsum('kfh,khd->kfd', hidden, w_down, precision=HIGH))
    head_in = rms_norm(output, norm_gains[:, 2:3, :])
    logits = low_back(jnp.einsum('kfd,kdv->kfv', low(head_in), w_head, precision=HIGH))
    log_total = jax.nn.logsumexp(logits, axis=-1)
    target_logit = jnp.take_along_axis(logits, by_pos[:, :, None], axis=2)[:, :, 0]
    return jnp.sum((log_total - target_logit) * loss_mask.T)

def reference(context, codes, delays, counts, w_attn_in, w_attn_out, w_gate_up, w_down, w_head, embed_table, norm_gains, first_attn_in, first_attn_out, first_gate_up, first_down, first_head, first_embed, first_gains, second_attn_in, second_attn_out, second_gate_up, second_down, second_head, second_embed, second_gains):
    params = (w_attn_in, w_attn_out, w_gate_up, w_down, w_head, embed_table, norm_gains)
    firsts = (first_attn_in, first_attn_out, first_gate_up, first_down, first_head, first_embed, first_gains)
    seconds = (second_attn_in, second_attn_out, second_gate_up, second_down, second_head, second_embed, second_gains)
    frames = context.shape[0]
    block = math.gcd(frames, 2048)
    blocks = frames // block
    targets = pick_targets(codes, delays)
    position = lax.broadcasted_iota(jnp.int32, targets.shape, 1)
    loss_mask = (position < counts[:, None]).astype(jnp.float32)
    total_count = jnp.sum(counts).astype(jnp.float32)
    context_blocks = context.reshape(blocks, block, context.shape[1])
    target_blocks = targets.reshape(blocks, block, targets.shape[1])
    mask_blocks = loss_mask.reshape(blocks, block, loss_mask.shape[1])

    def total_loss(weights):

        def one_block(carry, pieces):
            return (carry + jax.checkpoint(block_loss)(weights, pieces[0], pieces[1], pieces[2]), None)
        summed, _ = lax.scan(one_block, jnp.float32(0.0), (context_blocks, target_blocks, mask_blocks))
        return summed / total_count
    loss, pullback = jax.vjp(total_loss, params)
    grads = pullback(jnp.ones_like(loss))[0]
    grad_norm = jnp.sqrt(sum((jnp.sum(grad * grad) for grad in grads)))
    clip_scale = jnp.minimum(1.0, CLIP_NORM / (grad_norm + 1e-06))
    rates = (RATE_MATRIX,) * 5 + (RATE_TABLE, RATE_TABLE)
    new_weights, new_firsts, new_seconds = ([], [], [])
    for weight, first, second, grad, rate in zip(params, firsts, seconds, grads, rates):
        clipped = grad * clip_scale
        first_new = BETA_ONE * first + (1.0 - BETA_ONE) * clipped
        second_new = BETA_TWO * second + (1.0 - BETA_TWO) * clipped * clipped
        adam_step = first_new / BIAS_ONE / (jnp.sqrt(second_new / BIAS_TWO) + ADAM_EPS)
        new_weights.append(weight * (1.0 - rate * DECAY) - rate * adam_step)
        new_firsts.append(first_new)
        new_seconds.append(second_new)
    return (new_weights[0], new_weights[1], new_weights[2], new_weights[3], new_weights[4], new_weights[5], new_weights[6], new_firsts[0], new_firsts[1], new_firsts[2], new_firsts[3], new_firsts[4], new_firsts[5], new_firsts[6], new_seconds[0], new_seconds[1], new_seconds[2], new_seconds[3], new_seconds[4], new_seconds[5], new_seconds[6], loss, grad_norm)
```

```python
import jax
import jax.numpy as jnp
from jax import lax
from jax.sharding import PartitionSpec as P

HEAD_DIM = 64
TP = 4
LANE = 128

NORM_EPS = 1e-05
CLIP_NORM = 0.02
BETA_ONE = 0.9
BETA_TWO = 0.95
BIAS_ONE = 1.0 - 0.9**10
BIAS_TWO = 1.0 - 0.95**10
ADAM_EPS = 1e-08
DECAY = 0.1
RATE_MATRIX = 0.03
RATE_TABLE = 0.5

BF = jnp.bfloat16
F32 = jnp.float32


def core_swap(piece):
    return lax.ppermute(piece, "mp", [(0, 1), (1, 0)])


def flip(piece, mask):
    ways = lax.axis_size("dp")
    return lax.ppermute(piece, "dp", [(chip, chip ^ mask) for chip in range(ways)])


def peer(piece, step):
    return flip(piece, (step >> 1) * 4 + (step & 1))


def other_y(piece):
    return flip(piece, 2)


def from_h(piece, step):
    ways = lax.axis_size("dp")
    return lax.ppermute(piece, "dp", [(chip, (chip - 8 * step) % ways) for chip in range(ways)])


def to_h(piece, step):
    ways = lax.axis_size("dp")
    return lax.ppermute(piece, "dp", [(chip, (chip + 8 * step) % ways) for chip in range(ways)])


def group_gather(block):
    return jnp.concatenate([block] + [peer(block, step) for step in range(1, TP)], axis=0)


def group_scatter(partial):
    rows = partial.shape[0] // TP
    total = partial[:rows]
    for step in range(1, TP):
        total = total + peer(partial[step * rows : (step + 1) * rows].astype(BF), step).astype(F32)
    return total


def peer_slots(stats, step):
    parts = jnp.split(stats, TP, axis=1)
    return jnp.concatenate([parts[k ^ step] for k in range(TP)], axis=1)


def by_core(core, zero, one):
    return jnp.where(core == 0, zero, one)


def by_slot(rel, low, side):
    rel = [jnp.where(side == 0, rel[k], rel[k ^ 1]) for k in range(TP)]
    return [jnp.where(low == 0, rel[k], rel[k ^ 2]) for k in range(TP)]


def gather_weight(packed, core, low, side):
    mine = by_core(core, packed[0], packed[1])
    theirs = core_swap(by_core(core, packed[1], packed[0]))
    first = by_core(core, mine, theirs)
    second = by_core(core, theirs, mine)
    pieces = [first[0], first[1], second[0], second[1]]
    rel = by_slot(pieces, low, side)
    rel = [rel[0]] + [peer(rel[step], step) for step in range(1, TP)]
    held = jnp.concatenate(by_slot(rel, low, side), axis=0)
    groups = lax.axis_size("dp") // 8
    held = jnp.concatenate([held] + [from_h(held, step) for step in range(1, groups)], axis=0)
    return jnp.concatenate([held, other_y(held)], axis=0)


def scatter_grad(grad, core, low, side):
    half = grad.shape[0] // 2
    kept = grad[:half] + other_y(grad[half:].astype(BF)).astype(F32)
    groups = lax.axis_size("dp") // 8
    rows = half // groups
    total = kept[:rows]
    for step in range(1, groups):
        total = total + to_h(kept[step * rows : (step + 1) * rows].astype(BF), step).astype(F32)
    squares = jnp.sum(total * total)
    low_total = total.astype(BF).reshape(TP, rows // TP, -1)
    rel = by_slot([low_total[k] for k in range(TP)], low, side)
    rel = [rel[0]] + [peer(rel[step], step) for step in range(1, TP)]
    first, second = [jnp.stack(pair) for pair in zip(*[iter(by_slot(rel, low, side))] * 2)]
    mine = by_core(core, first, second)
    theirs = core_swap(by_core(core, second, first))
    return by_core(core, mine, theirs), by_core(core, theirs, mine), squares


def norm_parts(inputs):
    scale = lax.rsqrt(jnp.mean(inputs * inputs, axis=-1, keepdims=True) + NORM_EPS)
    return inputs * scale, scale


def norm_back(normed, scale, gain, upstream):
    scaled = upstream * gain
    inner = jnp.mean(scaled * normed, axis=-1, keepdims=True)
    return scale * (scaled - normed * inner), jnp.sum(upstream * normed, axis=0)


def dot(left, right):
    return jnp.dot(left, right, preferred_element_type=F32)


def dot_t(left, right):
    return lax.dot_general(left, right, (((1,), (1,)), ((), ())), preferred_element_type=F32)


def t_dot(left, right):
    return lax.dot_general(left, right, (((0,), (0,)), ((), ())), preferred_element_type=F32)


def wide_dot(left, right):
    return jnp.dot(left, right, preferred_element_type=F32, precision=lax.Precision.HIGHEST)


def split_hidden(array, wide):
    rest = array[..., wide:]
    pad = [(0, 0)] * (array.ndim - 1) + [(0, wide - rest.shape[-1])]
    return array[..., :wide], jnp.pad(rest, pad)


def halves(array):
    size = array.shape[-1] // 2
    return array[..., :size], array[..., size:]


def adam(weight, first, second, clipped, rate):
    first_new = BETA_ONE * first + (1.0 - BETA_ONE) * clipped
    second_new = BETA_TWO * second + (1.0 - BETA_TWO) * clipped * clipped
    adam_step = first_new / BIAS_ONE / (jnp.sqrt(second_new / BIAS_TWO) + ADAM_EPS)
    return weight * (1.0 - rate * DECAY) - rate * adam_step, first_new, second_new


def pick_targets(codes, delays):
    window = lax.broadcasted_iota(jnp.int32, (1, codes.shape[1], 1), 1)
    delayed = jnp.sum(jnp.where(window == delays[:, None, None], codes, 0), axis=1)
    position = lax.broadcasted_iota(jnp.int32, delayed.shape, 1)
    return jnp.where(position == 0, codes[:, 0, :], delayed)


def shards(*args):
    context, codes, delays, counts = args[:4]
    params, firsts, seconds = args[4:11], args[11:18], args[18:25]
    w_attn_in, w_attn_out, w_gate_up, w_down, w_head, embed_table, norm_gains = params
    chips = lax.axis_size("dp")
    groups = chips // 8
    chip = lax.axis_index("dp")
    core = lax.axis_index("mp")
    side = chip & 1
    level = (chip >> 1) & 1
    low = (chip >> 2) & 1
    high = chip >> 3
    slot = low * 2 + side
    frames, width = context.shape
    rows = width // chips
    ffn_half = w_down.shape[1]
    ffn_wide = -(-ffn_half // (2 * LANE)) * LANE
    vocab_half = embed_table.shape[1]

    out_t = jnp.swapaxes(w_attn_out, 1, 2)
    down_t = jnp.swapaxes(w_down, 1, 2)

    def pack(parts):
        zero = jnp.concatenate([part[0].astype(BF) for part in parts], axis=-1)
        one = jnp.concatenate([part[1].astype(BF) for part in parts], axis=-1)
        return jnp.stack([zero, one], axis=1)

    attn_parts = [halves(w_attn_in[:, :, k]) for k in range(3)] + [halves(out_t)]
    full_attn = gather_weight(pack(attn_parts), core, low, side)
    gate_parts = [split_hidden(w_gate_up[:, :, k], ffn_wide) for k in range(2)]
    full_gate = gather_weight(pack(gate_parts), core, low, side)
    full_down = gather_weight(pack([split_hidden(down_t, ffn_wide)]), core, low, side)
    full_head = gather_weight(pack([halves(w_head)]), core, low, side)
    heads_wide = w_attn_out.shape[1] // 2
    full_in, full_out = full_attn[:, : 3 * heads_wide], full_attn[:, 3 * heads_wide :]

    targets = pick_targets(codes, delays)
    facts = jnp.concatenate([targets.T, counts[None]], axis=0)
    facts = lax.all_to_all(jnp.broadcast_to(facts[None], (chips,) + facts.shape), "dp", 0, 0)
    gain_send = jnp.broadcast_to(
        norm_gains.astype(BF).reshape(1, 6, rows), (chips, 6, rows)
    )
    gain_all = lax.all_to_all(gain_send, "dp", 0, 0)
    total_count = jnp.sum(facts[:, 2]).astype(F32)
    inverse_count = 1.0 / total_count
    chip_ids = lax.broadcasted_iota(jnp.int32, (TP, chips), 1)
    steps = lax.broadcasted_iota(jnp.int32, (TP, chips), 0)
    slots = slot ^ steps
    members = high * 8 + (slots >> 1) * 4 + level * 2 + (slots & 1)
    chosen = (members == chip_ids)[:, :, None, None]
    group_facts = jnp.sum(jnp.where(chosen, facts[None], 0), axis=1)
    group_frames = TP * frames
    group_targets = by_core(core, group_facts[:, 0], group_facts[:, 1]).reshape(group_frames)
    group_mask = (group_facts[:, 2].reshape(group_frames) > core).astype(F32)

    feature = lax.broadcasted_iota(jnp.int32, (1, width), 1)
    member = feature // rows
    place_y = member // (groups * TP)
    place_h = (member // TP) % groups
    place_t = member % TP
    source_chip = (
        ((high + place_h) % groups) * 8
        + (place_t >> 1) * 4
        + (level ^ place_y) * 2
        + (place_t & 1)
    )
    source = source_chip * rows + feature % rows
    order = (lax.broadcasted_iota(jnp.int32, (width, width), 0) == source).astype(BF)

    vocab_ids = core * vocab_half + lax.broadcasted_iota(jnp.int32, (1, vocab_half), 1)
    all_hot = (facts[:, 0].reshape(-1, 1) == vocab_ids).astype(BF)
    looked = dot(all_hot, embed_table[0].astype(BF)).astype(BF)
    looked = looked + core_swap(looked)
    looked = lax.all_to_all(looked.reshape(chips, frames, rows), "dp", 0, 0)
    looked = jnp.swapaxes(looked, 0, 1).reshape(frames, width)
    gain_abs = jnp.swapaxes(gain_all, 0, 1).reshape(2, 3, width)
    gain_abs = by_core(core, gain_abs[0], gain_abs[1])
    base = by_core(core, context, looked)
    moved = dot(jnp.concatenate([base, gain_abs, jnp.zeros((13, width), BF)], axis=0), order)
    stream = moved[:frames]
    gains = moved[frames : frames + 3]

    attn_norm, attn_scale = norm_parts(stream)
    attn_low = group_gather((attn_norm * gains[0]).astype(BF))
    qkv = dot(attn_low, full_in).astype(BF)
    kv_other = core_swap(qkv[:, heads_wide:]).astype(F32)
    query = qkv[:, :heads_wide].astype(F32)
    key_self = qkv[:, heads_wide : 2 * heads_wide].astype(F32)
    val_self = qkv[:, 2 * heads_wide :].astype(F32)
    key_gap = kv_other[:, :heads_wide] - key_self
    val_gap = kv_other[:, heads_wide:] - val_self
    lane_row = lax.broadcasted_iota(jnp.int32, (heads_wide, heads_wide), 0) // HEAD_DIM
    lane_col = lax.broadcasted_iota(jnp.int32, (heads_wide, heads_wide), 1) // HEAD_DIM
    head_sum = (lane_row == lane_col).astype(F32)
    gap = wide_dot(query * key_gap, head_sum) * 0.125
    prob_other = by_core(core, 0.0, jax.nn.sigmoid(gap))
    prob_self = by_core(core, 1.0, jax.nn.sigmoid(-gap))
    attended = (val_self + prob_other * val_gap).astype(BF)
    residual = stream + group_scatter(dot_t(attended, full_out))
    ffn_norm, ffn_scale = norm_parts(residual)
    ffn_low = group_gather((ffn_norm * gains[1]).astype(BF))
    gate_up = dot(ffn_low, full_gate)
    gate, up = gate_up[:, :ffn_wide], gate_up[:, ffn_wide:]
    sig = jax.nn.sigmoid(gate)
    hidden = (gate * sig * up).astype(BF)
    output = residual + group_scatter(dot_t(hidden, full_down))
    head_norm, head_scale = norm_parts(output)
    head_low = group_gather((head_norm * gains[2]).astype(BF))
    logits = dot(head_low, full_head)
    vocab_part = logits.shape[1]
    part_ids = slot * vocab_part + lax.broadcasted_iota(jnp.int32, (1, vocab_part), 1)
    picks = group_targets[:, None] == part_ids
    part_max = jnp.max(logits, axis=-1)
    part_exp = jnp.exp(logits - part_max[:, None])
    part_sum = jnp.sum(part_exp, axis=-1)
    part_target = jnp.sum(jnp.where(picks, logits, 0.0), axis=-1)
    stats = jnp.stack([part_max, part_sum, part_target], axis=0)
    stats = [stats] + [peer_slots(peer(stats, step), step) for step in range(1, TP)]
    row_max = stats[0][0]
    for piece in stats[1:]:
        row_max = jnp.maximum(row_max, piece[0])
    sum_exp = sum(piece[1] * jnp.exp(piece[0] - row_max) for piece in stats)
    target_logit = sum(piece[2] for piece in stats)
    losses = (row_max + jnp.log(sum_exp) - target_logit) * group_mask
    loss_local = jnp.sum(losses[:frames])

    weight_row = group_mask * inverse_count
    factor = jnp.exp(part_max - row_max) / sum_exp
    d_logits = (
        (part_exp * factor[:, None] - picks.astype(F32)) * weight_row[:, None]
    ).astype(BF)
    d_head_in = group_scatter(dot_t(d_logits, full_head))
    grad_head = t_dot(head_low, d_logits)
    d_output, gain_head = norm_back(head_norm, head_scale, gains[2], d_head_in)
    d_output_low = group_gather(d_output.astype(BF))
    d_hidden = dot(d_output_low, full_down)
    d_gate = d_hidden * up * (sig * (1.0 + gate * (1.0 - sig)))
    d_up = d_hidden * (gate * sig)
    d_gate_up = jnp.concatenate([d_gate, d_up], axis=1).astype(BF)
    d_ffn_in = group_scatter(dot_t(d_gate_up, full_gate))
    grad_down = t_dot(d_output_low, hidden)
    grad_gate = t_dot(ffn_low, d_gate_up)
    d_norm_ffn, gain_ffn = norm_back(ffn_norm, ffn_scale, gains[1], d_ffn_in)
    d_residual = d_output + d_norm_ffn
    d_res_low = group_gather(d_residual.astype(BF))
    d_attended = dot(d_res_low, full_out)
    pull = wide_dot(d_attended * val_gap, head_sum)
    d_score = prob_other * prob_self * pull * 0.125
    d_query = d_score * key_gap
    d_key_other = d_score * query
    d_val_other = prob_other * d_attended
    d_kv = core_swap(jnp.concatenate([d_key_other, d_val_other], axis=1).astype(BF)).astype(F32)
    d_key = d_kv[:, :heads_wide] - d_key_other
    d_val = d_kv[:, heads_wide:] + prob_self * d_attended
    d_qkv = jnp.concatenate([d_query, d_key, d_val], axis=1).astype(BF)
    d_attn_in = group_scatter(dot_t(d_qkv, full_in))
    grad_attn = jnp.concatenate([t_dot(attn_low, d_qkv), t_dot(d_res_low, attended)], axis=1)
    d_norm_attn, gain_attn = norm_back(attn_norm, attn_scale, gains[0], d_attn_in)
    d_stream = (d_residual + d_norm_attn).astype(BF)

    gain_rows = jnp.stack([gain_attn, gain_ffn, gain_head]).astype(BF)
    back = jnp.concatenate([d_stream, gain_rows, jnp.zeros((13, width), BF)], axis=0)
    back = dot_t(back, order).astype(BF)
    back = jnp.swapaxes(back.reshape(frames + 16, chips, rows), 0, 1)
    back = lax.all_to_all(back, "dp", 0, 0)
    gain_mine = jnp.sum(back[:, frames : frames + 3].astype(F32), axis=0)
    back_other = core_swap(back)
    gain_theirs = jnp.sum(back_other[:, frames : frames + 3].astype(F32), axis=0)
    grad_gains = jnp.stack(
        [by_core(core, gain_mine, gain_theirs), by_core(core, gain_theirs, gain_mine)]
    )
    d_rows = by_core(core, back_other[:, :frames], back[:, :frames]).reshape(-1, rows)
    grad_embed = t_dot(all_hot, d_rows)

    head_zero, head_one, sq_head = scatter_grad(grad_head, core, low, side)
    down_zero, down_one, sq_down = scatter_grad(grad_down, core, low, side)
    gate_zero, gate_one, sq_gate = scatter_grad(grad_gate, core, low, side)
    attn_zero, attn_one, sq_attn = scatter_grad(grad_attn, core, low, side)
    squares = (
        sq_head
        + sq_down
        + sq_gate
        + sq_attn
        + jnp.sum(grad_embed * grad_embed)
        + jnp.sum(gain_mine * gain_mine)
    )
    tally_lane = lax.broadcasted_iota(jnp.int32, (8, LANE), 1)
    tally = jnp.where(tally_lane == 0, squares, jnp.where(tally_lane == 1, loss_local, 0.0))
    ways = chips * lax.axis_size("mp")
    tally = lax.all_to_all(jnp.broadcast_to(tally[None], (ways, 8, LANE)), ("dp", "mp"), 0, 0)
    tally = jnp.sum(tally[:, 0], axis=0)
    grad_norm = jnp.sqrt(tally[0])
    loss = tally[1] / total_count
    clip_scale = jnp.minimum(1.0, CLIP_NORM / (grad_norm + 1e-06))

    def unpack(zero, one, start, size):
        both = jnp.stack([zero[:, :, start : start + size], one[:, :, start : start + size]])
        return both[:, 0], both[:, 1]

    def join(parts):
        return jnp.concatenate(parts, axis=-1)

    def join_hidden(parts):
        return jnp.concatenate([parts[0], parts[1][..., : ffn_half - ffn_wide]], axis=-1)

    g_in = jnp.stack(
        [join(unpack(attn_zero, attn_one, k * heads_wide, heads_wide)) for k in range(3)], axis=2
    )
    g_out = jnp.swapaxes(join(unpack(attn_zero, attn_one, 3 * heads_wide, heads_wide)), 1, 2)
    g_gate = jnp.stack(
        [join_hidden(unpack(gate_zero, gate_one, k * ffn_wide, ffn_wide)) for k in range(2)], axis=2
    )
    g_down = jnp.swapaxes(join_hidden(unpack(down_zero, down_one, 0, ffn_wide)), 1, 2)
    g_head = join(unpack(head_zero, head_one, 0, vocab_part))
    grads = (g_in, g_out, g_gate, g_down, g_head, grad_embed[None], grad_gains)
    rates = (RATE_MATRIX,) * 5 + (RATE_TABLE, RATE_TABLE)
    updates = [
        adam(weight, first, second, grad.astype(F32) * clip_scale, rate)
        for weight, first, second, grad, rate in zip(params, firsts, seconds, grads, rates)
    ]
    new_weights, new_firsts, new_seconds = zip(*updates)
    return new_weights + new_firsts + new_seconds + (loss, grad_norm)


def solution(mesh):
    weight_specs = (
        P(None, "dp", None, "mp"),
        P(None, "mp", "dp"),
        P(None, "dp", None, "mp"),
        P(None, "mp", "dp"),
        P(None, "dp", "mp"),
        P(None, "mp", "dp"),
        P(None, None, "dp"),
    )
    in_specs = (P("dp", None), P("dp", None, None), P("dp"), P("dp")) + weight_specs * 3
    out_specs = weight_specs * 3 + (P(), P())
    return jax.shard_map(shards, mesh=mesh, in_specs=in_specs, out_specs=out_specs, check_vma=False)
```

```python
import jax
import jax.numpy as jnp
from jax import lax
from jax.sharding import PartitionSpec as P

HEAD_DIM = 64
TP = 4
LANE = 128

NORM_EPS = 1e-05
CLIP_NORM = 0.02
BETA_ONE = 0.9
BETA_TWO = 0.95
BIAS_ONE = 1.0 - 0.9**10
BIAS_TWO = 1.0 - 0.95**10
ADAM_EPS = 1e-08
DECAY = 0.1
RATE_MATRIX = 0.03
RATE_TABLE = 0.5

BF = jnp.bfloat16
F32 = jnp.float32


def core_swap(piece):
    return lax.ppermute(piece, "mp", [(0, 1), (1, 0)])


def flip(piece, mask):
    ways = lax.axis_size("dp")
    return lax.ppermute(piece, "dp", [(chip, chip ^ mask) for chip in range(ways)])


def peer(piece, step):
    return flip(piece, (step >> 1) * 4 + (step & 1))


def other_y(piece):
    return flip(piece, 2)


def from_h(piece, step):
    ways = lax.axis_size("dp")
    return lax.ppermute(piece, "dp", [(chip, (chip - 8 * step) % ways) for chip in range(ways)])


def to_h(piece, step):
    ways = lax.axis_size("dp")
    return lax.ppermute(piece, "dp", [(chip, (chip + 8 * step) % ways) for chip in range(ways)])


def group_gather(block):
    return jnp.concatenate([block] + [peer(block, step) for step in range(1, TP)], axis=0)


def group_scatter(partial):
    rows = partial.shape[0] // TP
    total = partial[:rows]
    for step in range(1, TP):
        total = total + peer(partial[step * rows : (step + 1) * rows].astype(BF), step).astype(F32)
    return total


def peer_slots(stats, step):
    parts = jnp.split(stats, TP, axis=1)
    return jnp.concatenate([parts[k ^ step] for k in range(TP)], axis=1)


def by_core(core, zero, one):
    return jnp.where(core == 0, zero, one)


def pick(array, index):
    return lax.dynamic_index_in_dim(array, index, 0, keepdims=False)


def both_halves(pack, core):
    mine = pack(core)
    theirs = core_swap(pack(1 - core))
    both = by_core(core, jnp.stack([mine, theirs]), jnp.stack([theirs, mine]))
    _, _, rows, columns = both.shape
    return both.reshape(TP, rows, columns)


def after(value, *earlier):
    return lax.optimization_barrier((value, earlier))[0]


def gather_weight(held):
    groups = lax.axis_size("dp") // 8
    near = [held] + [from_h(held, step) for step in range(1, groups)]
    return near + [other_y(block) for block in near]


def scatter_grad(blocks):
    groups = len(blocks) // 2
    nears = []
    for step in range(1, groups):
        nears.append(blocks[step] + other_y(blocks[groups + step].astype(BF)).astype(F32))
    total = blocks[0] + other_y(after(blocks[groups].astype(BF), nears)).astype(F32)
    for step, near in enumerate(nears, 1):
        total = total + to_h(near.astype(BF), step).astype(F32)
    return total, nears


def split_cores(parts, core):
    mine = pick(parts, core)
    theirs = core_swap(pick(parts, 1 - core))
    return by_core(core, mine, theirs), by_core(core, theirs, mine)


def peer_exchange(blocks, slot):
    rel = [pick(blocks, slot)] + [peer(pick(blocks, slot ^ step), step) for step in range(1, TP)]
    rel = [jnp.where(slot & 1 == 0, rel[k], rel[k ^ 1]) for k in range(TP)]
    return jnp.stack([jnp.where(slot & 2 == 0, rel[k], rel[k ^ 2]) for k in range(TP)])


def norm_parts(inputs):
    scale = lax.rsqrt(jnp.mean(inputs * inputs, axis=-1, keepdims=True) + NORM_EPS)
    return inputs * scale, scale


def norm_back(normed, scale, gain, upstream):
    scaled = upstream * gain
    inner = jnp.mean(scaled * normed, axis=-1, keepdims=True)
    return scale * (scaled - normed * inner), jnp.sum(upstream * normed, axis=0)


def dot(left, right):
    return jnp.dot(left, right, preferred_element_type=F32)


def dot_t(left, right):
    return lax.dot_general(left, right, (((1,), (1,)), ((), ())), preferred_element_type=F32)


def t_dot(left, right):
    return lax.dot_general(left, right, (((0,), (0,)), ((), ())), preferred_element_type=F32)


def wide_dot(left, right):
    return jnp.dot(left, right, preferred_element_type=F32, precision=lax.Precision.HIGHEST)


def split_hidden(array, wide):
    rest = array[..., wide:]
    pad = [(0, 0)] * (array.ndim - 1) + [(0, wide - rest.shape[-1])]
    return array[..., :wide], jnp.pad(rest, pad)


def halves(array):
    size = array.shape[-1] // 2
    return array[..., :size], array[..., size:]


def adam(weight, first, second, clipped, rate):
    first_new = BETA_ONE * first + (1.0 - BETA_ONE) * clipped
    second_new = BETA_TWO * second + (1.0 - BETA_TWO) * clipped * clipped
    adam_step = first_new / BIAS_ONE / (jnp.sqrt(second_new / BIAS_TWO) + ADAM_EPS)
    return weight * (1.0 - rate * DECAY) - rate * adam_step, first_new, second_new


def pick_targets(codes, delays):
    window = lax.broadcasted_iota(jnp.int32, (1, codes.shape[1], 1), 1)
    delayed = jnp.sum(jnp.where(window == delays[:, None, None], codes, 0), axis=1)
    position = lax.broadcasted_iota(jnp.int32, delayed.shape, 1)
    return jnp.where(position == 0, codes[:, 0, :], delayed)


def shards(*args):
    context, codes, delays, counts = args[:4]
    params, firsts, seconds = args[4:11], args[11:18], args[18:25]
    w_attn_in, w_attn_out, w_gate_up, w_down, w_head, embed_table, norm_gains = params
    chips = lax.axis_size("dp")
    groups = chips // 8
    chip = lax.axis_index("dp")
    core = lax.axis_index("mp")
    side = chip & 1
    level = (chip >> 1) & 1
    low = (chip >> 2) & 1
    high = chip >> 3
    slot = low * 2 + side
    frames, width = context.shape
    rows = width // chips
    ffn_half = w_down.shape[1]
    ffn_wide = -(-ffn_half // (2 * LANE)) * LANE
    vocab_half = embed_table.shape[1]

    out_t = jnp.swapaxes(w_attn_out, 1, 2)
    down_t = jnp.swapaxes(w_down, 1, 2)

    def pack(*parts):
        def packed(position):
            parted = [[pick(part, position).astype(BF) for part in pair] for pair in parts]
            return jnp.stack([jnp.concatenate(side_parts, axis=-1) for side_parts in zip(*parted)])

        return packed

    def concat_pack(*packs):
        return lambda position: jnp.concatenate([one(position) for one in packs], axis=-1)

    attn_pack = pack(*[halves(w_attn_in[:, :, k]) for k in range(3)], halves(out_t))
    attn_both = both_halves(attn_pack, core)
    attn_held = peer_exchange(attn_both, slot)

    targets = pick_targets(codes, delays)
    facts = jnp.concatenate([targets.T, counts[None]], axis=0).astype(F32)
    facts = jnp.concatenate([facts.reshape(1, -1), norm_gains.reshape(1, -1)], axis=1)
    facts = lax.all_to_all(
        jnp.broadcast_to(facts, (chips, facts.shape[1])), "dp", 0, 0, tiled=True
    )
    facts = after(facts, attn_both)
    gain_all = facts[:, 3 * frames :].reshape(chips, 6, rows).astype(BF)
    facts = facts[:, : 3 * frames].reshape(chips, 3, frames).astype(jnp.int32)

    gate_pack = pack(*[split_hidden(w_gate_up[:, :, k], ffn_wide) for k in range(2)])
    gate_both = both_halves(gate_pack, core)
    last_pack = concat_pack(pack(split_hidden(down_t, ffn_wide)), pack(halves(w_head)))
    last_both = both_halves(last_pack, core)
    heads_wide = w_attn_out.shape[1] // 2

    vocab_ids = core * vocab_half + lax.broadcasted_iota(jnp.int32, (1, vocab_half), 1)
    all_hot = (facts[:, 0].reshape(-1, 1) == vocab_ids).astype(BF)
    looked = dot(all_hot, embed_table[0].astype(BF)).astype(BF)
    looked = looked + core_swap(looked)
    looked = lax.all_to_all(after(looked, attn_held).reshape(chips, frames, rows), "dp", 0, 0)

    gate_held = peer_exchange(after(gate_both, attn_held), slot)
    last_held = peer_exchange(after(last_both, gate_held), slot)
    attn_blocks = gather_weight(attn_held.reshape(TP * rows, -1))
    gate_blocks = gather_weight(gate_held.reshape(TP * rows, -1))
    down_blocks = gather_weight(last_held[..., :ffn_wide].reshape(TP * rows, -1))
    head_blocks = gather_weight(last_held[..., ffn_wide:].reshape(TP * rows, -1))
    full_attn, full_gate, full_down, full_head = [
        jnp.concatenate(blocks) for blocks in (attn_blocks, gate_blocks, down_blocks, head_blocks)
    ]
    full_in, full_out = full_attn[:, : 3 * heads_wide], full_attn[:, 3 * heads_wide :]

    total_count = jnp.sum(facts[:, 2]).astype(F32)
    inverse_count = 1.0 / total_count
    chip_ids = lax.broadcasted_iota(jnp.int32, (TP, chips), 1)
    steps = lax.broadcasted_iota(jnp.int32, (TP, chips), 0)
    slots = slot ^ steps
    members = high * 8 + (slots >> 1) * 4 + level * 2 + (slots & 1)
    chosen = (members == chip_ids)[:, :, None, None]
    group_facts = jnp.sum(jnp.where(chosen, facts[None], 0), axis=1)
    group_frames = TP * frames
    group_targets = by_core(core, group_facts[:, 0], group_facts[:, 1]).reshape(group_frames)
    group_mask = (group_facts[:, 2].reshape(group_frames) > core).astype(F32)

    feature = lax.broadcasted_iota(jnp.int32, (1, width), 1)
    member = feature // rows
    place_y = member // (groups * TP)
    place_h = (member // TP) % groups
    place_t = member % TP
    source_chip = (
        ((high + place_h) % groups) * 8
        + (place_t >> 1) * 4
        + (level ^ place_y) * 2
        + (place_t & 1)
    )
    source = source_chip * rows + feature % rows
    order = (lax.broadcasted_iota(jnp.int32, (width, width), 0) == source).astype(BF)

    looked = jnp.swapaxes(looked, 0, 1).reshape(frames, width)
    gain_abs = jnp.swapaxes(gain_all, 0, 1).reshape(2, 3, width)
    gain_abs = by_core(core, gain_abs[0], gain_abs[1])
    base = by_core(core, context, looked)
    moved = dot(jnp.concatenate([base, gain_abs, jnp.zeros((13, width), BF)], axis=0), order)
    stream = moved[:frames]
    gains = moved[frames : frames + 3]

    attn_norm, attn_scale = norm_parts(stream)
    attn_low = group_gather((attn_norm * gains[0]).astype(BF))
    qkv = dot(attn_low, full_in).astype(BF)
    kv_other = core_swap(qkv[:, heads_wide:]).astype(F32)
    query = qkv[:, :heads_wide].astype(F32)
    key_self = qkv[:, heads_wide : 2 * heads_wide].astype(F32)
    val_self = qkv[:, 2 * heads_wide :].astype(F32)
    key_gap = kv_other[:, :heads_wide] - key_self
    val_gap = kv_other[:, heads_wide:] - val_self
    lane_row = lax.broadcasted_iota(jnp.int32, (heads_wide, heads_wide), 0) // HEAD_DIM
    lane_col = lax.broadcasted_iota(jnp.int32, (heads_wide, heads_wide), 1) // HEAD_DIM
    head_sum = (lane_row == lane_col).astype(F32)
    gap = wide_dot(query * key_gap, head_sum) * 0.125
    prob_other = by_core(core, 0.0, jax.nn.sigmoid(gap))
    prob_self = by_core(core, 1.0, jax.nn.sigmoid(-gap))
    attended = (val_self + prob_other * val_gap).astype(BF)
    residual = stream + group_scatter(dot_t(attended, full_out))
    ffn_norm, ffn_scale = norm_parts(residual)
    ffn_low = group_gather((ffn_norm * gains[1]).astype(BF))
    gate_up = dot(ffn_low, full_gate)
    gate, up = gate_up[:, :ffn_wide], gate_up[:, ffn_wide:]
    sig = jax.nn.sigmoid(gate)
    hidden = (gate * sig * up).astype(BF)
    output = residual + group_scatter(dot_t(hidden, full_down))
    head_norm, head_scale = norm_parts(output)
    head_low = group_gather((head_norm * gains[2]).astype(BF))
    logits = dot(head_low, full_head)
    vocab_part = logits.shape[1]
    part_ids = slot * vocab_part + lax.broadcasted_iota(jnp.int32, (1, vocab_part), 1)
    picks = group_targets[:, None] == part_ids
    part_max = jnp.max(logits, axis=-1)
    part_exp = jnp.exp(logits - part_max[:, None])
    part_sum = jnp.sum(part_exp, axis=-1)
    part_target = jnp.sum(jnp.where(picks, logits, 0.0), axis=-1)
    stats = jnp.stack([part_max, part_sum, part_target], axis=0)
    stats = [stats] + [peer_slots(peer(stats, step), step) for step in range(1, TP)]
    row_max = stats[0][0]
    for piece in stats[1:]:
        row_max = jnp.maximum(row_max, piece[0])
    sum_exp = sum(piece[1] * jnp.exp(piece[0] - row_max) for piece in stats)
    target_logit = sum(piece[2] for piece in stats)
    losses = (row_max + jnp.log(sum_exp) - target_logit) * group_mask
    loss_local = jnp.sum(losses[:frames])

    weight_row = group_mask * inverse_count
    factor = jnp.exp(part_max - row_max) / sum_exp
    d_logits = (
        (part_exp * factor[:, None] - picks.astype(F32)) * weight_row[:, None]
    ).astype(BF)
    d_head_in = group_scatter(dot_t(d_logits, full_head))
    grad_head = t_dot(head_low, d_logits)
    d_output, gain_head = norm_back(head_norm, head_scale, gains[2], d_head_in)
    d_output_low = group_gather(d_output.astype(BF))
    d_hidden = dot(d_output_low, full_down)
    d_gate = d_hidden * up * (sig * (1.0 + gate * (1.0 - sig)))
    d_up = d_hidden * (gate * sig)
    d_gate_up = jnp.concatenate([d_gate, d_up], axis=1).astype(BF)
    d_ffn_in = group_scatter(dot_t(d_gate_up, full_gate))
    grad_down = t_dot(d_output_low, hidden)
    grad_gate = t_dot(ffn_low, d_gate_up)
    d_norm_ffn, gain_ffn = norm_back(ffn_norm, ffn_scale, gains[1], d_ffn_in)
    d_residual = d_output + d_norm_ffn
    d_res_low = group_gather(d_residual.astype(BF))
    d_attended = dot(d_res_low, full_out)
    pull = wide_dot(d_attended * val_gap, head_sum)
    d_score = prob_other * prob_self * pull * 0.125
    d_query = d_score * key_gap
    d_key_other = d_score * query
    d_val_other = prob_other * d_attended
    d_kv = core_swap(jnp.concatenate([d_key_other, d_val_other], axis=1).astype(BF)).astype(F32)
    d_key = d_kv[:, :heads_wide] - d_key_other
    d_val = d_kv[:, heads_wide:] + prob_self * d_attended
    d_qkv = jnp.concatenate([d_query, d_key, d_val], axis=1).astype(BF)
    d_attn_in = group_scatter(dot_t(d_qkv, full_in))
    grad_attn = jnp.concatenate([t_dot(attn_low, d_qkv), t_dot(d_res_low, attended)], axis=1)
    d_norm_attn, gain_attn = norm_back(attn_norm, attn_scale, gains[0], d_attn_in)
    d_stream = (d_residual + d_norm_attn).astype(BF)

    returned = [
        scatter_grad(jnp.split(grad, 2 * groups))
        for grad in (grad_head, grad_down, grad_gate, grad_attn)
    ]
    sum_head, sum_down, sum_gate, sum_attn = [total for total, _ in returned]
    sq_head, sq_down, sq_gate, sq_attn = [jnp.sum(total * total) for total, _ in returned]
    sum_ffn = jnp.concatenate([sum_gate.astype(BF), sum_down.astype(BF), sum_head.astype(BF)], axis=1)
    sum_ffn = peer_exchange(sum_ffn.reshape(TP, rows, -1), slot)
    ffn_zero, ffn_one = split_cores(sum_ffn.reshape(2, 2, rows, -1), core)
    sum_attn = peer_exchange(sum_attn.astype(BF).reshape(TP, rows, -1), slot)
    attn_zero, attn_one = split_cores(sum_attn.reshape(2, 2, rows, -1), core)

    gain_rows = jnp.stack([gain_attn, gain_ffn, gain_head]).astype(BF)
    back = jnp.concatenate([d_stream, gain_rows, jnp.zeros((13, width), BF)], axis=0)
    back = dot_t(back, order).astype(BF)
    back = jnp.swapaxes(back.reshape(frames + 16, chips, rows), 0, 1)
    back = after(lax.all_to_all(back, "dp", 0, 0), returned[3][1])
    gain_mine = jnp.sum(back[:, frames : frames + 3].astype(F32), axis=0)
    back_other = core_swap(back)
    gain_theirs = jnp.sum(back_other[:, frames : frames + 3].astype(F32), axis=0)
    grad_gains = jnp.stack(
        [by_core(core, gain_mine, gain_theirs), by_core(core, gain_theirs, gain_mine)]
    )
    d_rows = by_core(core, back_other[:, :frames], back[:, :frames]).reshape(-1, rows)
    grad_embed = t_dot(all_hot, d_rows)
    squares = (
        sq_head
        + sq_down
        + sq_gate
        + sq_attn
        + jnp.sum(grad_embed * grad_embed)
        + jnp.sum(gain_mine * gain_mine)
    )
    tally_lane = lax.broadcasted_iota(jnp.int32, (8, LANE), 1)
    tally = jnp.where(tally_lane == 0, squares, jnp.where(tally_lane == 1, loss_local, 0.0))
    ways = chips * lax.axis_size("mp")
    tally = lax.all_to_all(jnp.broadcast_to(tally[None], (ways, 8, LANE)), ("dp", "mp"), 0, 0)
    tally = jnp.sum(tally[:, 0], axis=0)
    grad_norm = jnp.sqrt(tally[0])
    loss = tally[1] / total_count
    clip_scale = jnp.minimum(1.0, CLIP_NORM / (grad_norm + 1e-06))

    def unpack(zero, one, start, size):
        both = jnp.stack([zero[:, :, start : start + size], one[:, :, start : start + size]])
        return both[:, 0], both[:, 1]

    def join(parts):
        return jnp.concatenate(parts, axis=-1)

    def join_hidden(parts):
        return jnp.concatenate([parts[0], parts[1][..., : ffn_half - ffn_wide]], axis=-1)

    g_in = jnp.stack(
        [join(unpack(attn_zero, attn_one, k * heads_wide, heads_wide)) for k in range(3)], axis=2
    )
    g_out = jnp.swapaxes(join(unpack(attn_zero, attn_one, 3 * heads_wide, heads_wide)), 1, 2)
    g_gate = jnp.stack(
        [join_hidden(unpack(ffn_zero, ffn_one, k * ffn_wide, ffn_wide)) for k in range(2)], axis=2
    )
    g_down = jnp.swapaxes(join_hidden(unpack(ffn_zero, ffn_one, 2 * ffn_wide, ffn_wide)), 1, 2)
    g_head = join(unpack(ffn_zero, ffn_one, 3 * ffn_wide, vocab_part))
    grads = (g_in, g_out, g_gate, g_down, g_head, grad_embed[None], grad_gains)
    rates = (RATE_MATRIX,) * 5 + (RATE_TABLE, RATE_TABLE)
    updates = [
        adam(weight, first, second, grad.astype(F32) * clip_scale, rate)
        for weight, first, second, grad, rate in zip(params, firsts, seconds, grads, rates)
    ]
    new_weights, new_firsts, new_seconds = zip(*updates)
    return new_weights + new_firsts + new_seconds + (loss, grad_norm)


def solution(mesh):
    weight_specs = (
        P(None, "dp", None, "mp"),
        P(None, "mp", "dp"),
        P(None, "dp", None, "mp"),
        P(None, "mp", "dp"),
        P(None, "dp", "mp"),
        P(None, "mp", "dp"),
        P(None, None, "dp"),
    )
    in_specs = (P("dp", None), P("dp", None, None), P("dp"), P("dp")) + weight_specs * 3
    out_specs = weight_specs * 3 + (P(), P())
    return jax.shard_map(shards, mesh=mesh, in_specs=in_specs, out_specs=out_specs, check_vma=False)
```

```python
import jax
import jax.numpy as jnp
from jax import lax
from jax.experimental.layout import Layout, with_layout_constraint
from jax.sharding import PartitionSpec as P

HEAD_DIM = 64
TP = 4
LANE = 128

NORM_EPS = 1e-05
CLIP_NORM = 0.02
BETA_ONE = 0.9
BETA_TWO = 0.95
BIAS_ONE = 1.0 - 0.9**10
BIAS_TWO = 1.0 - 0.95**10
ADAM_EPS = 1e-08
DECAY = 0.1
RATE_MATRIX = 0.03
RATE_TABLE = 0.5

DEADLINES = [
    ("attn_b", "known"),
    ("gate_t", "last_x"),
    ("g_attn_y", "embedded"),
    ("g_head_y", "head_y0"),
    ("g_down_y", "down_y0"),
    ("g_gate_y", "gate_y0"),
    ("g_attn_y", "attn_y0"),
    ("down_z", "ffn"),
    ("last_t", "head"),
]

BF = jnp.bfloat16
F32 = jnp.float32


def core_swap(piece):
    return lax.ppermute(piece, "mp", [(0, 1), (1, 0)])


def flip(piece, mask):
    ways = lax.axis_size("dp")
    return lax.ppermute(piece, "dp", [(chip, chip ^ mask) for chip in range(ways)])


def peer(piece, step):
    return flip(piece, (step >> 1) * 4 + (step & 1))


def other_y(piece):
    return flip(piece, 2)


def from_h(piece, step):
    ways = lax.axis_size("dp")
    return lax.ppermute(piece, "dp", [(chip, (chip - 8 * step) % ways) for chip in range(ways)])


def to_h(piece, step):
    ways = lax.axis_size("dp")
    return lax.ppermute(piece, "dp", [(chip, (chip + 8 * step) % ways) for chip in range(ways)])


def group_gather(block):
    return jnp.concatenate([block] + [peer(block, step) for step in range(1, TP)], axis=0)


def group_scatter(partial):
    rows = partial.shape[0] // TP
    total = partial[:rows]
    for step in range(1, TP):
        total = total + peer(partial[step * rows : (step + 1) * rows].astype(BF), step).astype(F32)
    return total


def peer_slots(stats, step):
    parts = jnp.split(stats, TP, axis=1)
    return jnp.concatenate([parts[k ^ step] for k in range(TP)], axis=1)


def by_core(core, zero, one):
    return jnp.where(core == 0, zero, one)


def pick(array, index):
    return lax.dynamic_index_in_dim(array, index, 0, keepdims=False)


def both_halves(pack, core):
    mine = pack(core)
    theirs = core_swap(pack(1 - core))
    both = by_core(core, jnp.stack([mine, theirs]), jnp.stack([theirs, mine]))
    _, _, rows, columns = both.shape
    return both.reshape(TP, rows, columns)


def after(value, *earlier):
    return lax.optimization_barrier((value, earlier))[0]


def hook(ready, step, value):
    early = [ready[name] for name, place in DEADLINES if place == step]
    return after(value, *early) if early else value


def gather_weight(ready, name, held):
    groups = lax.axis_size("dp") // 8
    near = [held] + [from_h(held, step) for step in range(1, groups)]
    far = [other_y(block) for block in near]
    ready[name + "_h"], ready[name + "_y"], ready[name + "_z"] = near[1:], far[0], far[1:]
    return near + far


def scatter_grad(ready, name, blocks):
    groups = len(blocks) // 2
    nears = []
    for step in range(1, groups):
        nears.append(blocks[step] + other_y(blocks[groups + step].astype(BF)).astype(F32))
    ready["g_" + name + "_y"] = nears
    sent = hook(ready, name + "_y0", blocks[groups].astype(BF))
    total = blocks[0] + other_y(sent).astype(F32)
    ready["g_" + name + "_z"] = total
    for step, near in enumerate(nears, 1):
        total = total + to_h(near.astype(BF), step).astype(F32)
    ready["g_" + name + "_h"] = total
    return total


def split_cores(parts, core):
    mine = pick(parts, core)
    theirs = core_swap(pick(parts, 1 - core))
    return by_core(core, mine, theirs), by_core(core, theirs, mine)


def peer_exchange(blocks, slot):
    rel = [pick(blocks, slot)] + [peer(pick(blocks, slot ^ step), step) for step in range(1, TP)]
    rel = [jnp.where(slot & 1 == 0, rel[k], rel[k ^ 1]) for k in range(TP)]
    return jnp.stack([jnp.where(slot & 2 == 0, rel[k], rel[k ^ 2]) for k in range(TP)])


def norm_parts(inputs):
    scale = lax.rsqrt(jnp.mean(inputs * inputs, axis=-1, keepdims=True) + NORM_EPS)
    return inputs * scale, scale


def norm_back(normed, scale, gain, upstream):
    scaled = upstream * gain
    inner = jnp.mean(scaled * normed, axis=-1, keepdims=True)
    return scale * (scaled - normed * inner), jnp.sum(upstream * normed, axis=0)


def dot(left, right):
    return jnp.dot(left, right, preferred_element_type=F32)


def dot_t(left, right):
    return lax.dot_general(left, right, (((1,), (1,)), ((), ())), preferred_element_type=F32)


def t_dot(left, right):
    return lax.dot_general(left, right, (((0,), (0,)), ((), ())), preferred_element_type=F32)


def wide_dot(left, right):
    return jnp.dot(left, right, preferred_element_type=F32, precision=lax.Precision.HIGHEST)


def split_hidden(array, wide):
    rest = array[..., wide:]
    pad = [(0, 0)] * (array.ndim - 1) + [(0, wide - rest.shape[-1])]
    return array[..., :wide], jnp.pad(rest, pad)


def halves(array):
    size = array.shape[-1] // 2
    return array[..., :size], array[..., size:]


def adam(weight, first, second, clipped, rate):
    first_new = BETA_ONE * first + (1.0 - BETA_ONE) * clipped
    second_new = BETA_TWO * second + (1.0 - BETA_TWO) * clipped * clipped
    adam_step = first_new / BIAS_ONE / (jnp.sqrt(second_new / BIAS_TWO) + ADAM_EPS)
    return weight * (1.0 - rate * DECAY) - rate * adam_step, first_new, second_new


def pick_targets(codes, delays):
    window = lax.broadcasted_iota(jnp.int32, (1, codes.shape[1], 1), 1)
    delayed = jnp.sum(jnp.where(window == delays[:, None, None], codes, 0), axis=1)
    position = lax.broadcasted_iota(jnp.int32, delayed.shape, 1)
    return jnp.where(position == 0, codes[:, 0, :], delayed)


def shards(*args):
    context, codes, delays, counts = args[:4]
    params, firsts, seconds = args[4:11], args[11:18], args[18:25]
    w_attn_in, w_attn_out, w_gate_up, w_down, w_head, embed_table, norm_gains = params
    ready = {}
    chips = lax.axis_size("dp")
    groups = chips // 8
    chip = lax.axis_index("dp")
    core = lax.axis_index("mp")
    side = chip & 1
    level = (chip >> 1) & 1
    low = (chip >> 2) & 1
    high = chip >> 3
    slot = low * 2 + side
    frames, width = context.shape
    rows = width // chips
    ffn_half = w_down.shape[1]
    ffn_wide = -(-ffn_half // (2 * LANE)) * LANE
    vocab_half = embed_table.shape[1]

    out_t = jnp.swapaxes(w_attn_out, 1, 2)
    down_t = jnp.swapaxes(w_down, 1, 2)

    def pack(*parts):
        def packed(position):
            parted = [[pick(part, position).astype(BF) for part in pair] for pair in parts]
            return jnp.stack([jnp.concatenate(side_parts, axis=-1) for side_parts in zip(*parted)])

        return packed

    def concat_pack(*packs):
        return lambda position: jnp.concatenate([one(position) for one in packs], axis=-1)

    attn_pack = pack(*[halves(w_attn_in[:, :, k]) for k in range(3)], halves(out_t))
    attn_both = both_halves(attn_pack, core)
    attn_held = peer_exchange(attn_both, slot)
    ready["attn_b"], ready["attn_t"] = attn_both, attn_held

    targets = pick_targets(codes, delays)
    facts = jnp.concatenate([targets.T, counts[None]], axis=0).astype(F32)
    facts = jnp.concatenate([facts.reshape(1, -1), norm_gains.reshape(1, -1)], axis=1)
    facts = lax.all_to_all(
        jnp.broadcast_to(hook(ready, "facts", facts), (chips, facts.shape[1])), "dp", 0, 0, tiled=True
    )
    facts = hook(ready, "known", facts)
    gain_all = facts[:, 3 * frames :].reshape(chips, 6, rows).astype(BF)
    facts = facts[:, : 3 * frames].reshape(chips, 3, frames).astype(jnp.int32)

    gate_pack = pack(*[split_hidden(w_gate_up[:, :, k], ffn_wide) for k in range(2)])
    gate_both = both_halves(gate_pack, core)
    last_pack = concat_pack(pack(split_hidden(down_t, ffn_wide)), pack(halves(w_head)))
    last_both = both_halves(last_pack, core)
    heads_wide = w_attn_out.shape[1] // 2

    gate_held = peer_exchange(hook(ready, "gate_x", gate_both), slot)
    ready["gate_t"] = gate_held
    last_held = peer_exchange(hook(ready, "last_x", last_both), slot)
    ready["last_t"] = last_held
    attn_blocks = gather_weight(ready, "attn", attn_held.reshape(TP * rows, -1))
    gate_blocks = gather_weight(ready, "gate", gate_held.reshape(TP * rows, -1))
    down_blocks = gather_weight(ready, "down", last_held[..., :ffn_wide].reshape(TP * rows, -1))
    head_blocks = gather_weight(ready, "head", last_held[..., ffn_wide:].reshape(TP * rows, -1))

    vocab_ids = core * vocab_half + lax.broadcasted_iota(jnp.int32, (1, vocab_half), 1)
    all_hot = (facts[:, 0].reshape(-1, 1) == vocab_ids).astype(BF)
    looked = dot(all_hot, embed_table[0].astype(BF)).astype(BF)
    looked = looked + core_swap(looked)
    looked = lax.all_to_all(hook(ready, "looked", looked).reshape(chips, frames, rows), "dp", 0, 0)

    full_attn, full_gate, full_down, full_head = [
        jnp.concatenate(blocks) for blocks in (attn_blocks, gate_blocks, down_blocks, head_blocks)
    ]
    full_in, full_out = full_attn[:, : 3 * heads_wide], full_attn[:, 3 * heads_wide :]

    total_count = jnp.sum(facts[:, 2]).astype(F32)
    inverse_count = 1.0 / total_count
    chip_ids = lax.broadcasted_iota(jnp.int32, (TP, chips), 1)
    steps = lax.broadcasted_iota(jnp.int32, (TP, chips), 0)
    slots = slot ^ steps
    members = high * 8 + (slots >> 1) * 4 + level * 2 + (slots & 1)
    chosen = (members == chip_ids)[:, :, None, None]
    group_facts = jnp.sum(jnp.where(chosen, facts[None], 0), axis=1)
    group_frames = TP * frames
    group_targets = by_core(core, group_facts[:, 0], group_facts[:, 1]).reshape(group_frames)
    group_mask = (group_facts[:, 2].reshape(group_frames) > core).astype(F32)

    feature = lax.broadcasted_iota(jnp.int32, (1, width), 1)
    member = feature // rows
    place_y = member // (groups * TP)
    place_h = (member // TP) % groups
    place_t = member % TP
    source_chip = (
        ((high + place_h) % groups) * 8
        + (place_t >> 1) * 4
        + (level ^ place_y) * 2
        + (place_t & 1)
    )
    source = source_chip * rows + feature % rows
    order = (lax.broadcasted_iota(jnp.int32, (width, width), 0) == source).astype(BF)

    looked = jnp.swapaxes(looked, 0, 1).reshape(frames, width)
    gain_abs = jnp.swapaxes(gain_all, 0, 1).reshape(2, 3, width)
    gain_abs = by_core(core, gain_abs[0], gain_abs[1])
    base = by_core(core, context, looked)
    moved = dot(jnp.concatenate([base, gain_abs, jnp.zeros((13, width), BF)], axis=0), order)
    stream = moved[:frames]
    gains = moved[frames : frames + 3]

    attn_norm, attn_scale = norm_parts(hook(ready, "norm", stream))
    attn_low = group_gather((attn_norm * gains[0]).astype(BF))
    qkv = dot(hook(ready, "qkv", attn_low), full_in).astype(BF)
    kv_other = core_swap(qkv[:, heads_wide:]).astype(F32)
    query = hook(ready, "attend", qkv[:, :heads_wide]).astype(F32)
    key_self = qkv[:, heads_wide : 2 * heads_wide].astype(F32)
    val_self = qkv[:, 2 * heads_wide :].astype(F32)
    key_gap = kv_other[:, :heads_wide] - key_self
    val_gap = kv_other[:, heads_wide:] - val_self
    lane_row = lax.broadcasted_iota(jnp.int32, (heads_wide, heads_wide), 0) // HEAD_DIM
    lane_col = lax.broadcasted_iota(jnp.int32, (heads_wide, heads_wide), 1) // HEAD_DIM
    head_sum = (lane_row == lane_col).astype(F32)
    gap = wide_dot(query * key_gap, head_sum) * 0.125
    prob_other = by_core(core, 0.0, jax.nn.sigmoid(gap))
    prob_self = by_core(core, 1.0, jax.nn.sigmoid(-gap))
    attended = (val_self + prob_other * val_gap).astype(BF)
    residual = hook(ready, "add1", stream) + group_scatter(dot_t(attended, full_out))
    ffn_norm, ffn_scale = norm_parts(residual)
    ffn_low = group_gather((ffn_norm * gains[1]).astype(BF))
    gate_up = dot(hook(ready, "ffn", ffn_low), full_gate)
    gate, up = gate_up[:, :ffn_wide], gate_up[:, ffn_wide:]
    sig = jax.nn.sigmoid(gate)
    hidden = (gate * sig * up).astype(BF)
    output = hook(ready, "add2", residual) + group_scatter(dot_t(hook(ready, "down", hidden), full_down))
    head_norm, head_scale = norm_parts(output)
    head_low = group_gather((head_norm * gains[2]).astype(BF))
    logits = dot(hook(ready, "head", head_low), full_head)
    vocab_part = logits.shape[1]
    part_ids = slot * vocab_part + lax.broadcasted_iota(jnp.int32, (1, vocab_part), 1)
    picks = group_targets[:, None] == part_ids
    part_max = jnp.max(logits, axis=-1)
    part_exp = jnp.exp(logits - part_max[:, None])
    part_sum = jnp.sum(part_exp, axis=-1)
    part_target = jnp.sum(jnp.where(picks, logits, 0.0), axis=-1)
    stats = jnp.stack([part_max, part_sum, part_target], axis=0)
    stats = [stats] + [peer_slots(peer(stats, step), step) for step in range(1, TP)]
    row_max = stats[0][0]
    for piece in stats[1:]:
        row_max = jnp.maximum(row_max, piece[0])
    sum_exp = sum(piece[1] * jnp.exp(piece[0] - row_max) for piece in stats)
    target_logit = sum(piece[2] for piece in stats)
    losses = (row_max + jnp.log(sum_exp) - target_logit) * group_mask
    loss_local = jnp.sum(losses[:frames])

    weight_row = group_mask * inverse_count
    factor = jnp.exp(part_max - row_max) / sum_exp
    d_logits = (
        (part_exp * factor[:, None] - picks.astype(F32)) * weight_row[:, None]
    ).astype(BF)
    d_head_in = group_scatter(dot_t(d_logits, full_head))
    def by_blocks(left, right):
        return [t_dot(part, right) for part in jnp.split(left, 2 * groups, axis=1)]

    grad_head = lax.optimization_barrier(by_blocks(head_low, d_logits))
    sum_head = scatter_grad(ready, "head", grad_head)
    d_output, gain_head = norm_back(
        head_norm, head_scale, gains[2], hook(ready, "back1", d_head_in)
    )
    d_output_low = group_gather(d_output.astype(BF))
    d_hidden = dot(hook(ready, "dffn", d_output_low), full_down)
    d_gate = d_hidden * up * (sig * (1.0 + gate * (1.0 - sig)))
    d_up = d_hidden * (gate * sig)
    d_gate_up = jnp.concatenate([d_gate, d_up], axis=1).astype(BF)
    d_ffn_in = group_scatter(dot_t(d_gate_up, full_gate))
    sum_down = scatter_grad(ready, "down", by_blocks(d_output_low, hidden))
    sum_gate = scatter_grad(ready, "gate", by_blocks(ffn_low, d_gate_up))
    d_norm_ffn, gain_ffn = norm_back(
        ffn_norm, ffn_scale, gains[1], hook(ready, "back2", d_ffn_in)
    )
    d_residual = d_output + d_norm_ffn
    d_res_low = group_gather(d_residual.astype(BF))
    d_attended = dot(hook(ready, "datt", d_res_low), full_out)
    pull = wide_dot(d_attended * val_gap, head_sum)
    d_score = prob_other * prob_self * pull * 0.125
    d_query = d_score * key_gap
    d_key_other = d_score * query
    d_val_other = prob_other * d_attended
    d_kv = core_swap(
        hook(ready, "swap", jnp.concatenate([d_key_other, d_val_other], axis=1).astype(BF))
    ).astype(F32)
    d_key = d_kv[:, :heads_wide] - d_key_other
    d_val = d_kv[:, heads_wide:] + prob_self * d_attended
    d_qkv = jnp.concatenate([d_query, d_key, d_val], axis=1).astype(BF)
    d_attn_in = group_scatter(dot_t(hook(ready, "dqkv", d_qkv), full_in))
    grad_attn = [
        jnp.concatenate(pair, axis=1)
        for pair in zip(by_blocks(attn_low, d_qkv), by_blocks(d_res_low, attended))
    ]
    sum_attn = scatter_grad(ready, "attn", grad_attn)
    d_norm_attn, gain_attn = norm_back(
        attn_norm, attn_scale, gains[0], hook(ready, "back3", d_attn_in)
    )
    d_stream = (d_residual + d_norm_attn).astype(BF)

    sums = [sum_head, sum_down, sum_gate, sum_attn]
    sq_head, sq_down, sq_gate, sq_attn = [jnp.sum(total * total) for total in sums]
    sum_ffn = jnp.concatenate([sum_gate.astype(BF), sum_down.astype(BF), sum_head.astype(BF)], axis=1)
    sum_ffn = hook(ready, "sumffn", sum_ffn)
    sum_ffn = peer_exchange(sum_ffn.reshape(TP, rows, -1), slot)
    ffn_zero, ffn_one = split_cores(sum_ffn.reshape(2, 2, rows, -1), core)
    sum_attn = peer_exchange(sum_attn.astype(BF).reshape(TP, rows, -1), slot)
    attn_zero, attn_one = split_cores(sum_attn.reshape(2, 2, rows, -1), core)

    gain_rows = jnp.stack([gain_attn, gain_ffn, gain_head]).astype(BF)
    d_stream = hook(ready, "embed", d_stream)
    back = jnp.concatenate([d_stream, gain_rows, jnp.zeros((13, width), BF)], axis=0)
    back = dot_t(back, order).astype(BF)
    back = jnp.swapaxes(back.reshape(frames + 16, chips, rows), 0, 1)
    back = hook(ready, "embedded", lax.all_to_all(back, "dp", 0, 0))
    gain_mine = jnp.sum(back[:, frames : frames + 3].astype(F32), axis=0)
    back_other = core_swap(back)
    gain_theirs = jnp.sum(back_other[:, frames : frames + 3].astype(F32), axis=0)
    grad_gains = jnp.stack(
        [by_core(core, gain_mine, gain_theirs), by_core(core, gain_theirs, gain_mine)]
    )
    d_rows = by_core(core, back_other[:, :frames], back[:, :frames]).reshape(-1, rows)
    grad_embed = t_dot(all_hot, d_rows)
    squares = (
        sq_head
        + sq_down
        + sq_gate
        + sq_attn
        + jnp.sum(grad_embed * grad_embed)
        + jnp.sum(gain_mine * gain_mine)
    )
    tally_lane = lax.broadcasted_iota(jnp.int32, (8, LANE), 1)
    tally = jnp.where(tally_lane == 0, squares, jnp.where(tally_lane == 1, loss_local, 0.0))
    ways = chips * lax.axis_size("mp")
    tally = lax.all_to_all(jnp.broadcast_to(tally[None], (ways, 8, LANE)), ("dp", "mp"), 0, 0)
    tally = jnp.sum(tally[:, 0], axis=0)
    grad_norm = jnp.sqrt(tally[0])
    loss = tally[1] / total_count
    clip_scale = jnp.minimum(1.0, CLIP_NORM / (grad_norm + 1e-06))

    def unpack(zero, one, start, size):
        both = jnp.stack([zero[:, :, start : start + size], one[:, :, start : start + size]])
        return both[:, 0], both[:, 1]

    def join(parts):
        return jnp.concatenate(parts, axis=-1)

    def join_hidden(parts):
        return jnp.concatenate([parts[0], parts[1][..., : ffn_half - ffn_wide]], axis=-1)

    g_in = jnp.stack(
        [join(unpack(attn_zero, attn_one, k * heads_wide, heads_wide)) for k in range(3)], axis=2
    )
    g_out = jnp.swapaxes(join(unpack(attn_zero, attn_one, 3 * heads_wide, heads_wide)), 1, 2)
    g_gate = jnp.stack(
        [join_hidden(unpack(ffn_zero, ffn_one, k * ffn_wide, ffn_wide)) for k in range(2)], axis=2
    )
    g_down = jnp.swapaxes(join_hidden(unpack(ffn_zero, ffn_one, 2 * ffn_wide, ffn_wide)), 1, 2)
    g_head = join(unpack(ffn_zero, ffn_one, 3 * ffn_wide, vocab_part))
    g_in = with_layout_constraint(g_in, Layout((0, 2, 1, 3)))
    g_gate = with_layout_constraint(g_gate, Layout((0, 1, 2, 3)))
    grads = (g_in, g_out, g_gate, g_down, g_head, grad_embed[None], grad_gains)
    rates = (RATE_MATRIX,) * 5 + (RATE_TABLE, RATE_TABLE)
    updates = [
        adam(weight, first, second, grad.astype(F32) * clip_scale, rate)
        for weight, first, second, grad, rate in zip(params, firsts, seconds, grads, rates)
    ]
    new_weights, new_firsts, new_seconds = zip(*updates)
    return new_weights + new_firsts + new_seconds + (loss, grad_norm)


def solution(mesh):
    weight_specs = (
        P(None, "dp", None, "mp"),
        P(None, "mp", "dp"),
        P(None, "dp", None, "mp"),
        P(None, "mp", "dp"),
        P(None, "dp", "mp"),
        P(None, "mp", "dp"),
        P(None, None, "dp"),
    )
    in_specs = (P("dp", None), P("dp", None, None), P("dp"), P("dp")) + weight_specs * 3
    out_specs = weight_specs * 3 + (P(), P())
    return jax.shard_map(shards, mesh=mesh, in_specs=in_specs, out_specs=out_specs, check_vma=False)
```

```python
import jax
import jax.numpy as jnp
from jax import lax
from jax.experimental.layout import Layout, with_layout_constraint
from jax.sharding import PartitionSpec as P

HEAD_DIM = 64
TP = 4
LANE = 128

NORM_EPS = 1e-05
CLIP_NORM = 0.02
BETA_ONE = 0.9
BETA_TWO = 0.95
BIAS_ONE = 1.0 - 0.9**10
BIAS_TWO = 1.0 - 0.95**10
ADAM_EPS = 1e-08
DECAY = 0.1
RATE_MATRIX = 0.03
RATE_TABLE = 0.5

DEADLINES = [
    ("attn_b", "known"),
    ("gate_t", "last_x"),
    ("g_attn_y", "embedded"),
    ("g_head_y", "head_y0"),
    ("g_down_y", "down_y0"),
    ("g_gate_y", "gate_y0"),
    ("g_attn_y", "attn_y0"),
    ("down_z", "ffn"),
    ("last_t", "head"),
]

BF = jnp.bfloat16
F32 = jnp.float32


def core_swap(piece):
    return lax.ppermute(piece, "mp", [(0, 1), (1, 0)])


def flip(piece, mask):
    ways = lax.axis_size("dp")
    return lax.ppermute(piece, "dp", [(chip, chip ^ mask) for chip in range(ways)])


def peer(piece, step):
    return flip(piece, (step >> 1) * 4 + (step & 1))


def other_y(piece):
    return flip(piece, 2)


def from_h(piece, step):
    ways = lax.axis_size("dp")
    return lax.ppermute(piece, "dp", [(chip, (chip - 8 * step) % ways) for chip in range(ways)])


def to_h(piece, step):
    ways = lax.axis_size("dp")
    return lax.ppermute(piece, "dp", [(chip, (chip + 8 * step) % ways) for chip in range(ways)])


def group_gather(block):
    return jnp.concatenate([block] + [peer(block, step) for step in range(1, TP)], axis=0)


def group_scatter(partial):
    rows = partial.shape[0] // TP
    total = partial[:rows]
    for step in range(1, TP):
        total = total + peer(partial[step * rows : (step + 1) * rows].astype(BF), step).astype(F32)
    return total


def peer_slots(stats, step):
    parts = jnp.split(stats, TP, axis=1)
    return jnp.concatenate([parts[k ^ step] for k in range(TP)], axis=1)


def by_core(core, zero, one):
    return jnp.where(core == 0, zero, one)


def pick(array, index):
    return lax.dynamic_index_in_dim(array, index, 0, keepdims=False)


def both_halves(pack, core):
    mine = pack(core)
    theirs = core_swap(pack(1 - core))
    both = by_core(core, jnp.stack([mine, theirs]), jnp.stack([theirs, mine]))
    _, _, rows, columns = both.shape
    return both.reshape(TP, rows, columns)


def after(value, *earlier):
    return lax.optimization_barrier((value, earlier))[0]


def hook(ready, step, value):
    early = [ready[name] for name, place in DEADLINES if place == step]
    return after(value, *early) if early else value


def gather_weight(ready, name, held):
    groups = lax.axis_size("dp") // 8
    near = [held] + [from_h(held, step) for step in range(1, groups)]
    far = [other_y(block) for block in near]
    ready[name + "_h"], ready[name + "_y"], ready[name + "_z"] = near[1:], far[0], far[1:]
    return near + far


def scatter_grad(ready, name, blocks):
    groups = len(blocks) // 2
    nears = []
    for step in range(1, groups):
        nears.append(blocks[step] + other_y(blocks[groups + step].astype(BF)).astype(F32))
    ready["g_" + name + "_y"] = nears
    sent = hook(ready, name + "_y0", blocks[groups].astype(BF))
    total = blocks[0] + other_y(sent).astype(F32)
    ready["g_" + name + "_z"] = total
    for step, near in enumerate(nears, 1):
        total = total + to_h(near.astype(BF), step).astype(F32)
    ready["g_" + name + "_h"] = total
    return total


def split_cores(parts, core):
    mine = pick(parts, core)
    theirs = core_swap(pick(parts, 1 - core))
    return by_core(core, mine, theirs), by_core(core, theirs, mine)


def peer_exchange(blocks, slot):
    rel = [pick(blocks, slot)] + [peer(pick(blocks, slot ^ step), step) for step in range(1, TP)]
    rel = [jnp.where(slot & 1 == 0, rel[k], rel[k ^ 1]) for k in range(TP)]
    return jnp.stack([jnp.where(slot & 2 == 0, rel[k], rel[k ^ 2]) for k in range(TP)])


def norm_parts(inputs):
    scale = lax.rsqrt(jnp.mean(inputs * inputs, axis=-1, keepdims=True) + NORM_EPS)
    return inputs * scale, scale


def norm_back(normed, scale, gain, upstream):
    scaled = upstream * gain
    inner = jnp.mean(scaled * normed, axis=-1, keepdims=True)
    return scale * (scaled - normed * inner), jnp.sum(upstream * normed, axis=0)


def dot(left, right):
    return jnp.dot(left, right, preferred_element_type=F32)


def dot_t(left, right):
    return lax.dot_general(left, right, (((1,), (1,)), ((), ())), preferred_element_type=F32)


def t_dot(left, right):
    return lax.dot_general(left, right, (((0,), (0,)), ((), ())), preferred_element_type=F32)


def wide_dot(left, right):
    return jnp.dot(left, right, preferred_element_type=F32, precision=lax.Precision.HIGHEST)


def split_hidden(array, wide):
    rest = array[..., wide:]
    pad = [(0, 0)] * (array.ndim - 1) + [(0, wide - rest.shape[-1])]
    return array[..., :wide], jnp.pad(rest, pad)


def halves(array):
    size = array.shape[-1] // 2
    return array[..., :size], array[..., size:]


def adam(weight, first, second, clipped, rate):
    first_new = BETA_ONE * first + (1.0 - BETA_ONE) * clipped
    second_new = BETA_TWO * second + (1.0 - BETA_TWO) * clipped * clipped
    adam_step = first_new / BIAS_ONE / (jnp.sqrt(second_new / BIAS_TWO) + ADAM_EPS)
    return weight * (1.0 - rate * DECAY) - rate * adam_step, first_new, second_new


def pick_targets(codes, delays):
    window = lax.broadcasted_iota(jnp.int32, (1, codes.shape[1], 1), 1)
    delayed = jnp.sum(jnp.where(window == delays[:, None, None], codes, 0), axis=1)
    position = lax.broadcasted_iota(jnp.int32, delayed.shape, 1)
    return jnp.where(position == 0, codes[:, 0, :], delayed)


def shards(*args):
    context, codes, delays, counts = args[:4]
    params, firsts, seconds = args[4:11], args[11:18], args[18:25]
    w_attn_in, w_attn_out, w_gate_up, w_down, w_head, embed_table, norm_gains = params
    ready = {}
    chips = lax.axis_size("dp")
    groups = chips // 8
    chip = lax.axis_index("dp")
    core = lax.axis_index("mp")
    side = chip & 1
    level = (chip >> 1) & 1
    low = (chip >> 2) & 1
    high = chip >> 3
    slot = low * 2 + side
    frames, width = context.shape
    rows = width // chips
    ffn_half = w_down.shape[1]
    ffn_wide = -(-ffn_half // (2 * LANE)) * LANE
    vocab_half = embed_table.shape[1]

    out_t = jnp.swapaxes(w_attn_out, 1, 2)
    down_t = jnp.swapaxes(w_down, 1, 2)

    def pack(*parts):
        def packed(position):
            parted = [[pick(part, position).astype(BF) for part in pair] for pair in parts]
            return jnp.stack([jnp.concatenate(side_parts, axis=-1) for side_parts in zip(*parted)])

        return packed

    def concat_pack(*packs):
        return lambda position: jnp.concatenate([one(position) for one in packs], axis=-1)

    attn_pack = pack(*[halves(w_attn_in[:, :, k]) for k in range(3)], halves(out_t))
    attn_both = both_halves(attn_pack, core)
    attn_held = peer_exchange(attn_both, slot)
    ready["attn_b"], ready["attn_t"] = attn_both, attn_held

    targets = pick_targets(codes, delays)
    facts = jnp.concatenate([targets.T, counts[None]], axis=0).astype(F32)
    facts = jnp.concatenate([facts.reshape(1, -1), norm_gains.reshape(1, -1)], axis=1)
    facts = lax.all_to_all(
        jnp.broadcast_to(hook(ready, "facts", facts), (chips, facts.shape[1])), "dp", 0, 0, tiled=True
    )
    facts = hook(ready, "known", facts)
    gain_all = facts[:, 3 * frames :].reshape(chips, 6, rows).astype(BF)
    facts = facts[:, : 3 * frames].reshape(chips, 3, frames).astype(jnp.int32)

    gate_pack = pack(*[split_hidden(w_gate_up[:, :, k], ffn_wide) for k in range(2)])
    gate_both = both_halves(gate_pack, core)
    last_pack = concat_pack(pack(split_hidden(down_t, ffn_wide)), pack(halves(w_head)))
    last_both = both_halves(last_pack, core)
    heads_wide = w_attn_out.shape[1] // 2

    gate_held = peer_exchange(hook(ready, "gate_x", gate_both), slot)
    ready["gate_t"] = gate_held
    last_held = peer_exchange(hook(ready, "last_x", last_both), slot)
    ready["last_t"] = last_held
    attn_blocks = gather_weight(ready, "attn", attn_held.reshape(TP * rows, -1))
    gate_blocks = gather_weight(ready, "gate", gate_held.reshape(TP * rows, -1))
    down_blocks = gather_weight(ready, "down", last_held[..., :ffn_wide].reshape(TP * rows, -1))
    head_blocks = gather_weight(ready, "head", last_held[..., ffn_wide:].reshape(TP * rows, -1))

    vocab_ids = core * vocab_half + lax.broadcasted_iota(jnp.int32, (1, vocab_half), 1)
    all_hot = (facts[:, 0].reshape(-1, 1) == vocab_ids).astype(BF)
    looked = dot(all_hot, embed_table[0].astype(BF)).astype(BF)
    looked = looked + core_swap(looked)
    looked = lax.all_to_all(hook(ready, "looked", looked).reshape(chips, frames, rows), "dp", 0, 0)

    full_attn, full_gate, full_down, full_head = [
        jnp.concatenate(blocks) for blocks in (attn_blocks, gate_blocks, down_blocks, head_blocks)
    ]
    full_in, full_out = full_attn[:, : 3 * heads_wide], full_attn[:, 3 * heads_wide :]

    total_count = jnp.sum(facts[:, 2]).astype(F32)
    inverse_count = 1.0 / total_count
    chip_ids = lax.broadcasted_iota(jnp.int32, (TP, chips), 1)
    steps = lax.broadcasted_iota(jnp.int32, (TP, chips), 0)
    slots = slot ^ steps
    members = high * 8 + (slots >> 1) * 4 + level * 2 + (slots & 1)
    chosen = (members == chip_ids)[:, :, None, None]
    group_facts = jnp.sum(jnp.where(chosen, facts[None], 0), axis=1)
    group_frames = TP * frames
    group_targets = by_core(core, group_facts[:, 0], group_facts[:, 1]).reshape(group_frames)
    group_mask = (group_facts[:, 2].reshape(group_frames) > core).astype(F32)

    feature = lax.broadcasted_iota(jnp.int32, (1, width), 1)
    member = feature // rows
    place_y = member // (groups * TP)
    place_h = (member // TP) % groups
    place_t = member % TP
    source_chip = (
        ((high + place_h) % groups) * 8
        + (place_t >> 1) * 4
        + (level ^ place_y) * 2
        + (place_t & 1)
    )
    source = source_chip * rows + feature % rows
    order = (lax.broadcasted_iota(jnp.int32, (width, width), 0) == source).astype(BF)

    looked = jnp.swapaxes(looked, 0, 1).reshape(frames, width)
    gain_abs = jnp.swapaxes(gain_all, 0, 1).reshape(2, 3, width)
    gain_abs = by_core(core, gain_abs[0], gain_abs[1])
    base = by_core(core, context, looked)
    moved = dot(jnp.concatenate([base, gain_abs, jnp.zeros((13, width), BF)], axis=0), order)
    stream = moved[:frames]
    gains = moved[frames : frames + 3]

    attn_norm, attn_scale = norm_parts(hook(ready, "norm", stream))
    attn_low = group_gather((attn_norm * gains[0]).astype(BF))
    qkv = dot(hook(ready, "qkv", attn_low), full_in).astype(BF)
    kv_other = core_swap(qkv[:, heads_wide:]).astype(F32)
    query = hook(ready, "attend", qkv[:, :heads_wide]).astype(F32)
    key_self = qkv[:, heads_wide : 2 * heads_wide].astype(F32)
    val_self = qkv[:, 2 * heads_wide :].astype(F32)
    key_gap = kv_other[:, :heads_wide] - key_self
    val_gap = kv_other[:, heads_wide:] - val_self
    lane_row = lax.broadcasted_iota(jnp.int32, (heads_wide, heads_wide), 0) // HEAD_DIM
    lane_col = lax.broadcasted_iota(jnp.int32, (heads_wide, heads_wide), 1) // HEAD_DIM
    head_sum = (lane_row == lane_col).astype(F32)
    gap = wide_dot(query * key_gap, head_sum) * 0.125
    prob_other = by_core(core, 0.0, jax.nn.sigmoid(gap))
    prob_self = by_core(core, 1.0, jax.nn.sigmoid(-gap))
    attended = (val_self + prob_other * val_gap).astype(BF)
    residual = hook(ready, "add1", stream) + group_scatter(dot_t(attended, full_out))
    ffn_norm, ffn_scale = norm_parts(residual)
    ffn_low = group_gather((ffn_norm * gains[1]).astype(BF))
    gate_up = dot(hook(ready, "ffn", ffn_low), full_gate)
    gate, up = gate_up[:, :ffn_wide], gate_up[:, ffn_wide:]
    sig = jax.nn.sigmoid(gate)
    hidden = (gate * sig * up).astype(BF)
    output = hook(ready, "add2", residual) + group_scatter(dot_t(hook(ready, "down", hidden), full_down))
    head_norm, head_scale = norm_parts(output)
    head_low = group_gather((head_norm * gains[2]).astype(BF))
    logits = dot(hook(ready, "head", head_low), full_head)
    vocab_part = logits.shape[1]
    part_ids = slot * vocab_part + lax.broadcasted_iota(jnp.int32, (1, vocab_part), 1)
    picks = group_targets[:, None] == part_ids
    part_max = jnp.max(logits, axis=-1)
    part_exp = jnp.exp(logits - part_max[:, None])
    part_sum = jnp.sum(part_exp, axis=-1)
    part_target = jnp.sum(jnp.where(picks, logits, 0.0), axis=-1)
    stats = jnp.stack([part_max, part_sum, part_target], axis=0)
    stats = [stats] + [peer_slots(peer(stats, step), step) for step in range(1, TP)]
    row_max = stats[0][0]
    for piece in stats[1:]:
        row_max = jnp.maximum(row_max, piece[0])
    sum_exp = sum(piece[1] * jnp.exp(piece[0] - row_max) for piece in stats)
    target_logit = sum(piece[2] for piece in stats)
    losses = (row_max + jnp.log(sum_exp) - target_logit) * group_mask
    loss_local = jnp.sum(losses[:frames])

    weight_row = group_mask * inverse_count
    factor = jnp.exp(part_max - row_max) / sum_exp
    d_logits = (
        (part_exp * factor[:, None] - picks.astype(F32)) * weight_row[:, None]
    ).astype(BF)
    d_head_in = group_scatter(dot_t(d_logits, full_head))
    def by_blocks(left, right):
        return [t_dot(part, right) for part in jnp.split(left, 2 * groups, axis=1)]

    grad_head = lax.optimization_barrier(by_blocks(head_low, d_logits))
    sum_head = scatter_grad(ready, "head", grad_head)
    d_output, gain_head = norm_back(
        head_norm, head_scale, gains[2], hook(ready, "back1", d_head_in)
    )
    d_output_low = group_gather(d_output.astype(BF))
    d_hidden = dot(hook(ready, "dffn", d_output_low), full_down)
    d_gate = d_hidden * up * (sig * (1.0 + gate * (1.0 - sig)))
    d_up = d_hidden * (gate * sig)
    d_gate_up = jnp.concatenate([d_gate, d_up], axis=1).astype(BF)
    d_ffn_in = group_scatter(dot_t(d_gate_up, full_gate))
    sum_down = scatter_grad(ready, "down", by_blocks(d_output_low, hidden))
    sum_gate = scatter_grad(ready, "gate", by_blocks(ffn_low, d_gate_up))
    d_norm_ffn, gain_ffn = norm_back(
        ffn_norm, ffn_scale, gains[1], hook(ready, "back2", d_ffn_in)
    )
    d_residual = d_output + d_norm_ffn
    d_res_low = group_gather(d_residual.astype(BF))
    d_attended = dot(hook(ready, "datt", d_res_low), full_out)
    pull = wide_dot(d_attended * val_gap, head_sum)
    d_score = prob_other * prob_self * pull * 0.125
    d_query = d_score * key_gap
    d_key_other = d_score * query
    d_val_other = prob_other * d_attended
    d_kv = core_swap(
        hook(ready, "swap", jnp.concatenate([d_key_other, d_val_other], axis=1).astype(BF))
    ).astype(F32)
    d_key = d_kv[:, :heads_wide] - d_key_other
    d_val = d_kv[:, heads_wide:] + prob_self * d_attended
    d_qkv = jnp.concatenate([d_query, d_key, d_val], axis=1).astype(BF)
    d_attn_in = group_scatter(dot_t(hook(ready, "dqkv", d_qkv), full_in))
    grad_attn = [
        jnp.concatenate(pair, axis=1)
        for pair in zip(by_blocks(attn_low, d_qkv), by_blocks(d_res_low, attended))
    ]
    sum_attn = scatter_grad(ready, "attn", grad_attn)
    d_norm_attn, gain_attn = norm_back(
        attn_norm, attn_scale, gains[0], hook(ready, "back3", d_attn_in)
    )
    d_stream = (d_residual + d_norm_attn).astype(BF)

    sums = [sum_head, sum_down, sum_gate, sum_attn]
    sq_head, sq_down, sq_gate, sq_attn = [jnp.sum(total * total) for total in sums]
    sum_ffn = jnp.concatenate([sum_gate.astype(BF), sum_down.astype(BF), sum_head.astype(BF)], axis=1)
    sum_ffn = hook(ready, "sumffn", sum_ffn)
    sum_ffn = peer_exchange(sum_ffn.reshape(TP, rows, -1), slot)
    ffn_zero, ffn_one = split_cores(sum_ffn.reshape(2, 2, rows, -1), core)
    sum_attn = peer_exchange(sum_attn.astype(BF).reshape(TP, rows, -1), slot)
    attn_zero, attn_one = split_cores(sum_attn.reshape(2, 2, rows, -1), core)

    gain_rows = jnp.stack([gain_attn, gain_ffn, gain_head]).astype(BF)
    d_stream = hook(ready, "embed", d_stream)
    back = jnp.concatenate([d_stream, gain_rows, jnp.zeros((13, width), BF)], axis=0)
    back = dot_t(back, order).astype(BF)
    back = jnp.swapaxes(back.reshape(frames + 16, chips, rows), 0, 1)
    back = hook(ready, "embedded", lax.all_to_all(back, "dp", 0, 0))
    gain_mine = jnp.sum(back[:, frames : frames + 3].astype(F32), axis=0)
    back_other = core_swap(back)
    gain_theirs = jnp.sum(back_other[:, frames : frames + 3].astype(F32), axis=0)
    grad_gains = jnp.stack(
        [by_core(core, gain_mine, gain_theirs), by_core(core, gain_theirs, gain_mine)]
    )
    d_rows = by_core(core, back_other[:, :frames], back[:, :frames]).reshape(-1, rows)
    grad_embed = t_dot(all_hot, d_rows)
    squares = (
        sq_head
        + sq_down
        + sq_gate
        + sq_attn
        + jnp.sum(grad_embed * grad_embed)
        + jnp.sum(gain_mine * gain_mine)
    )
    tally_lane = lax.broadcasted_iota(jnp.int32, (1, LANE), 1)
    tally = jnp.where(tally_lane == 0, squares, jnp.where(tally_lane == 1, loss_local, 0.0))
    ways = chips * lax.axis_size("mp")
    tally = lax.all_to_all(jnp.broadcast_to(tally[None], (ways, 1, LANE)), ("dp", "mp"), 0, 0)
    tally = jnp.sum(tally[:, 0], axis=0)
    grad_norm = jnp.sqrt(tally[0])
    loss = tally[1] / total_count
    clip_scale = jnp.minimum(1.0, CLIP_NORM / (grad_norm + 1e-06))

    def unpack(zero, one, start, size):
        both = jnp.stack([zero[:, :, start : start + size], one[:, :, start : start + size]])
        return both[:, 0], both[:, 1]

    def join(parts):
        return jnp.concatenate(parts, axis=-1)

    def join_hidden(parts):
        return jnp.concatenate([parts[0], parts[1][..., : ffn_half - ffn_wide]], axis=-1)

    g_in = jnp.stack(
        [join(unpack(attn_zero, attn_one, k * heads_wide, heads_wide)) for k in range(3)], axis=2
    )
    g_out = jnp.swapaxes(join(unpack(attn_zero, attn_one, 3 * heads_wide, heads_wide)), 1, 2)
    g_gate = jnp.stack(
        [join_hidden(unpack(ffn_zero, ffn_one, k * ffn_wide, ffn_wide)) for k in range(2)], axis=2
    )
    g_down = jnp.swapaxes(join_hidden(unpack(ffn_zero, ffn_one, 2 * ffn_wide, ffn_wide)), 1, 2)
    g_head = join(unpack(ffn_zero, ffn_one, 3 * ffn_wide, vocab_part))
    g_in = with_layout_constraint(g_in, Layout((0, 2, 1, 3)))
    g_gate = with_layout_constraint(g_gate, Layout((0, 1, 2, 3)))
    grads = (g_in, g_out, g_gate, g_down, g_head, grad_embed[None], grad_gains)
    rates = (RATE_MATRIX,) * 5 + (RATE_TABLE, RATE_TABLE)
    updates = [
        adam(weight, first, second, grad.astype(F32) * clip_scale, rate)
        for weight, first, second, grad, rate in zip(params, firsts, seconds, grads, rates)
    ]
    new_weights, new_firsts, new_seconds = zip(*updates)
    return new_weights + new_firsts + new_seconds + (loss, grad_norm)


def solution(mesh):
    weight_specs = (
        P(None, "dp", None, "mp"),
        P(None, "mp", "dp"),
        P(None, "dp", None, "mp"),
        P(None, "mp", "dp"),
        P(None, "dp", "mp"),
        P(None, "mp", "dp"),
        P(None, None, "dp"),
    )
    in_specs = (P("dp", None), P("dp", None, None), P("dp"), P("dp")) + weight_specs * 3
    out_specs = weight_specs * 3 + (P(), P())
    return jax.shard_map(shards, mesh=mesh, in_specs=in_specs, out_specs=out_specs, check_vma=False)
```
